512 devices in a mesh: seq: 64 (over x, y_lo, z), aud: 8 (over y_hi, core).
Axes of the slice: x: 4, y: 8 (y_hi: 4, y_lo: 2; y = y_hi * 2 + y_lo), z: 8, core: 2. Of those that a mesh axis runs over, the one named last changes fastest.
Arguments:
- video_query: bfloat16 [8192, 2048], P('seq', 'aud'), may hold values from -9 to 9
- video_key: bfloat16 [8192, 2048], P('seq', 'aud'), may hold values from -9 to 9
- video_value: bfloat16 [8192, 2048], P('seq', 'aud'), may hold values from -6 to 6
- audio_query: bfloat16 [512, 2048], P('aud'), may hold values from -9 to 9
- audio_key: bfloat16 [512, 2048], P('aud'), may hold values from -9 to 9
- audio_value: bfloat16 [512, 2048], P('aud'), may hold values from -6 to 6
- video_grad: bfloat16 [8192, 2048], P('seq', 'aud'), may hold values from -6 to 6
- audio_grad: bfloat16 [512, 2048], P('aud'), may hold values from -6 to 6
- block_list: int32 [64, 3], P('seq'), may hold values from 0 to 3, as said below
- block_count: int32 [64], P('seq'), may hold values from 1 to 3, as said below
Outputs:
- video_out: bfloat16 [8192, 2048], P('seq', 'aud')
- audio_out: bfloat16 [512, 2048], P('aud')
- grad_audio_query: bfloat16 [512, 2048], P('aud')
- grad_audio_key: bfloat16 [512, 2048], P('aud')
- grad_audio_value: bfloat16 [512, 2048], P('aud')
The draws below stay inside these ranges and needn't reach their ends.
Inputs may be any that keep to these rules, and one draw needn't show every extreme that they name: `block_list`: row b lists in rising order the audio blocks of 128 tokens that intersect video block b in time or lie next to that span; only the first block_count[b] entries count and the others repeat the first; every audio block is listed by some row. `block_count`: some row counts 3 entries.
All inputs are finite; a program needn't handle non-finite values.
Results may differ from the reference program's by a relative error of at most 0.01325.
The reference program's roundings to bfloat16 on the way count: a program that leaves them out, or rounds other values in their place, can miss the bound.
Values may be sent and summed in bfloat16 or wider, within the bound.
No kernel may reach another device: no remote copies, remote signals or barrier semaphores. Data moves between devices by JAX's collectives and lax.ppermute only.
A program may use at most 192 MiB of HBM per device.

```python
import math
import jax
import jax.numpy as jnp
from jax import lax

HEADS = 16
HEAD_DIM = 128
BLOCK = 128
VIDEO_TOKENS = 8192
AUDIO_TOKENS = 512
VIDEO_BLOCKS = 64
AUDIO_BLOCKS = 4
MOST = 3


def shared_pattern(key):
    return jnp.where(jax.random.bernoulli(key, 0.5, (HEADS * HEAD_DIM,)), 1.0, -1.0).astype(jnp.float32)


def entries_rows(key, count):
    return jnp.clip(jax.random.normal(key, (count, HEADS * HEAD_DIM), jnp.float32), -4.5, 4.5)


def top_level():
    return math.sqrt(230.0 / math.sqrt(HEAD_DIM))


def key_level():
    return 9.0


def notch_depth():
    return 2.0 * math.sqrt(HEAD_DIM) / (top_level() * key_level())


def plant_rows(drawn_rows, pattern, period, offset, height, lowering, notch):
    index_rows = jnp.arange(drawn_rows.shape[0])
    chosen = index_rows % period == offset
    level = height * (1.0 - lowering * (index_rows * 7 % 5).astype(jnp.float32) / 4.0)
    column_ids = jnp.arange(drawn_rows.shape[1])
    shaped = pattern * (1.0 - notch * (column_ids % HEAD_DIM == 0).astype(jnp.float32))
    return jnp.where(chosen[:, None], level[:, None] * shaped[None, :], drawn_rows)


def base_rows(key, count):
    return entries_rows(key, count)


def intersection_lists(key):
    key = jax.random.fold_in(key, 97)
    block_ids = jnp.arange(VIDEO_BLOCKS)
    centre = (2 * block_ids + 1) * AUDIO_BLOCKS // (2 * VIDEO_BLOCKS)
    reach = jax.random.randint(key, (2, VIDEO_BLOCKS), 0, 2)
    middle = block_ids == VIDEO_BLOCKS // 2
    reach = jnp.where(middle[None, :], 1, reach)
    lowest = jnp.maximum(centre - reach[0], 0)
    highest = jnp.minimum(centre + reach[1], AUDIO_BLOCKS - 1)
    counts = highest - lowest + 1
    slot_ids = jnp.arange(MOST)
    listed = jnp.where(slot_ids[None, :] < counts[:, None], lowest[:, None] + slot_ids[None, :], lowest[:, None])
    return (listed.astype(jnp.int32), counts.astype(jnp.int32))


def draw_video_query(key, part):
    pattern = shared_pattern(key)
    key = jax.random.fold_in(key, 11)
    return plant_rows(base_rows(key, VIDEO_TOKENS), pattern, 61, 7, top_level(), 0.25, 0.0).astype(jnp.bfloat16)


def draw_video_key(key, part):
    pattern = shared_pattern(key)
    key = jax.random.fold_in(key, 12)
    drawn_rows = plant_rows(base_rows(key, VIDEO_TOKENS), pattern, 61, 7, key_level(), 0.0, 0.0)
    return plant_rows(drawn_rows, pattern, 61, 8, key_level(), 0.0, notch_depth()).astype(jnp.bfloat16)


def draw_audio_query(key, part):
    pattern = shared_pattern(key)
    key = jax.random.fold_in(key, 13)
    return plant_rows(base_rows(key, AUDIO_TOKENS), pattern, 29, 3, top_level(), 0.25, 0.0).astype(jnp.bfloat16)


def draw_audio_key(key, part):
    pattern = shared_pattern(key)
    key = jax.random.fold_in(key, 14)
    drawn_rows = plant_rows(base_rows(key, AUDIO_TOKENS), pattern, 29, 3, key_level(), 0.0, 0.0)
    return plant_rows(drawn_rows, pattern, 29, 4, key_level(), 0.0, notch_depth()).astype(jnp.bfloat16)


def draw_block_list(key, part):
    listed, counts = intersection_lists(key)
    return listed


def draw_block_count(key, part):
    listed, counts = intersection_lists(key)
    return counts


def levels(stream_key, extent, cuts, smallest, high):
    level, own = 1.0, jax.random.fold_in(stream_key, 6)
    for position, parts in cuts:
        heights = jnp.exp(jax.random.uniform(jax.random.fold_in(own, position), (parts,), jnp.float32, smallest / len(cuts), high / len(cuts)))
        level = level * jnp.repeat(heights, extent[position] // parts).reshape([-1 if axis == position else 1 for axis in range(len(extent))])
    return level


def bell_draw(stream_key, extent, spread, most, cuts=(), kind=jnp.bfloat16):
    level = levels(stream_key, extent, cuts, -0.22, 0.18) if cuts else 1.0
    result = jax.random.normal(stream_key, extent, jnp.float32) * spread * level
    return jnp.minimum(jnp.maximum(result, -most), most).astype(kind)


def setup_inputs(seed: int = 0) -> dict:
    key_of = jax.random.split(jax.random.key(seed), 11)
    video_query = draw_video_query(jax.random.fold_in(key_of[10], 71), 0)
    video_key = draw_video_key(jax.random.fold_in(key_of[10], 71), 0)
    video_value = bell_draw(key_of[2], (VIDEO_TOKENS, HEADS * HEAD_DIM), 1.0, 6.0, ((0, 64), (1, 8)))
    audio_query = draw_audio_query(jax.random.fold_in(key_of[10], 71), 0)
    audio_key = draw_audio_key(jax.random.fold_in(key_of[10], 71), 0)
    audio_value = bell_draw(key_of[5], (AUDIO_TOKENS, HEADS * HEAD_DIM), 1.0, 6.0, ((0, 8),))
    video_grad = bell_draw(key_of[6], (VIDEO_TOKENS, HEADS * HEAD_DIM), 1.0, 6.0, ((0, 64), (1, 8)))
    audio_grad = bell_draw(key_of[7], (AUDIO_TOKENS, HEADS * HEAD_DIM), 1.0, 6.0, ((0, 8),))
    block_list = draw_block_list(jax.random.fold_in(key_of[10], 71), 0)
    block_count = draw_block_count(jax.random.fold_in(key_of[10], 71), 0)
    return {"video_query": video_query, "video_key": video_key, "video_value": video_value, "audio_query": audio_query, "audio_key": audio_key, "audio_value": audio_value, "video_grad": video_grad, "audio_grad": audio_grad, "block_list": block_list, "block_count": block_count}


def heads_of(matrix):
    return jnp.transpose(matrix.reshape(matrix.shape[0], HEADS, HEAD_DIM), (1, 0, 2))

def joined(tensor):
    return jnp.transpose(tensor, (1, 0, 2)).reshape(tensor.shape[1], HEADS * HEAD_DIM)

def pair_tokens(block_list, block_count):
    slot_ids = jnp.arange(block_list.shape[1]).astype(jnp.int32)
    live_slots = slot_ids[None, :] < block_count[:, None]
    block_ids = jnp.arange(AUDIO_TOKENS // BLOCK).astype(jnp.int32)
    block_pairs = jnp.any(live_slots[:, :, None] & (block_list[:, :, None] == block_ids[None, None, :]), axis=1)
    return jnp.repeat(jnp.repeat(block_pairs, BLOCK, axis=0), BLOCK, axis=1)

def reference(video_query, video_key, video_value, audio_query, audio_key, audio_value, video_grad, audio_grad, block_list, block_count):
    score_scale = 1.0 / math.sqrt(HEAD_DIM)
    token_pairs = pair_tokens(block_list, block_count)
    back_pairs = token_pairs.T

    def self_head(operands):
        queries, keys, values = operands
        scores = jnp.dot(queries, keys.T, preferred_element_type=jnp.float32) * score_scale
        row_max = lax.optimization_barrier(jnp.max(scores, axis=1, keepdims=True))
        weights = jnp.exp(scores - row_max)
        row_total = lax.optimization_barrier(jnp.sum(weights, axis=1, keepdims=True))
        return jnp.dot(weights.astype(jnp.bfloat16), values, preferred_element_type=jnp.float32) / row_total

    def masked_head(queries, keys, values, upstream, allowed):
        scores = jnp.dot(queries, keys.T, preferred_element_type=jnp.float32) * score_scale
        row_max = lax.optimization_barrier(jnp.max(jnp.where(allowed, scores, -jnp.inf), axis=1, keepdims=True))
        weights = jnp.where(allowed, jnp.exp(scores - row_max), 0.0)
        row_total = lax.optimization_barrier(jnp.sum(weights, axis=1, keepdims=True))
        output = jnp.dot(weights.astype(jnp.bfloat16), values, preferred_element_type=jnp.float32) / row_total
        probs = weights / row_total
        dprobs = jnp.dot(upstream, values.T, preferred_element_type=jnp.float32)
        delta = lax.optimization_barrier(jnp.sum(upstream.astype(jnp.float32) * output, axis=1, keepdims=True))
        dscores = probs * (dprobs - delta)
        return (output, probs, dscores)

    def video_cross(operands):
        queries, keys, values, upstream = operands
        output, probs, dscores = masked_head(queries, keys, values, upstream, token_pairs)
        grad_values = jnp.dot(probs.astype(jnp.bfloat16).T, upstream, preferred_element_type=jnp.float32)
        grad_keys = jnp.dot(dscores.astype(jnp.bfloat16).T, queries, preferred_element_type=jnp.float32) * score_scale
        return (output, grad_keys, grad_values)

    def audio_cross(operands):
        queries, keys, values, upstream = operands
        output, probs, dscores = masked_head(queries, keys, values, upstream, back_pairs)
        grad_queries = jnp.dot(dscores.astype(jnp.bfloat16), keys, preferred_element_type=jnp.float32) * score_scale
        return (output, grad_queries)
    video_q = heads_of(video_query)
    video_k = heads_of(video_key)
    video_v = heads_of(video_value)
    self_out = lax.map(self_head, (video_q, video_k, video_v))
    cross_out, grad_key, grad_value = lax.map(video_cross, (video_q, heads_of(audio_key), heads_of(audio_value), heads_of(video_grad)))
    audio_attn, grad_query = lax.map(audio_cross, (heads_of(audio_query), video_k, video_v, heads_of(audio_grad)))
    video_out = joined(self_out + cross_out).astype(jnp.bfloat16)
    return (video_out, joined(audio_attn).astype(jnp.bfloat16), joined(grad_query).astype(jnp.bfloat16), joined(grad_key).astype(jnp.bfloat16), joined(grad_value).astype(jnp.bfloat16))
```

```python
import functools
import math

import jax
import jax.numpy as jnp
from jax import lax
from jax.experimental import pallas as pl
from jax.experimental.pallas import tpu as pltpu
from jax.sharding import Mesh, PartitionSpec as P

HEAD_DIM = 128
ROWS = ("x", "yl")
COLS = ("z",)
AUD = ("yh", "core")
SEQ = ROWS + COLS
SCALE = 1.0 / math.sqrt(HEAD_DIM)
bf16 = jnp.bfloat16
f32 = jnp.float32
VMEM_LIMIT = 20 * 1024 * 1024
PACK = 528
CHUNK = 32
SENT = 160


VM = pl.BlockSpec(memory_space=pltpu.VMEM)
SM = pl.BlockSpec(memory_space=pltpu.SMEM)
HBM = pl.BlockSpec(memory_space=pl.ANY)


def call(
    kernel, outs, flops, scratch=(), smem=0, args=(), in_specs=None, out_specs=None, limit=VMEM_LIMIT
):
    return pl.pallas_call(
        kernel,
        out_shape=[jax.ShapeDtypeStruct(s, d) for s, d in outs],
        in_specs=in_specs or [SM] * smem + [VM] * (len(args) - smem),
        out_specs=out_specs or [VM] * len(outs),
        scratch_shapes=list(scratch),
        compiler_params=pltpu.CompilerParams(vmem_limit_bytes=limit),
        cost_estimate=pl.CostEstimate(flops=flops, bytes_accessed=4000000, transcendentals=0),
    )(*args)


def dot_t(left, right):
    return lax.dot_general(left, right, (((1,), (1,)), ((), ())), preferred_element_type=f32)


def dot_n(left, right):
    return lax.dot_general(left, right, (((1,), (0,)), ((), ())), preferred_element_type=f32)


def dot_tn(left, right):
    return lax.dot_general(left, right, (((0,), (0,)), ((), ())), preferred_element_type=f32)


def pack_video(list_ref, count_ref, *rest):
    ins, (out_ref, twice_ref), (held, marks, sems) = rest[:4], rest[4:6], rest[6:]
    loads = [
        pltpu.make_async_copy(ref, held.at[place], sems.at[place])
        for place, ref in enumerate(ins)
    ]
    for load in loads:
        load.start()
    lanes = lax.broadcasted_iota(jnp.int32, (16, 256), 1)
    block = (lanes % 64) // 16
    allow = jnp.zeros((16, 256), f32)
    for slot in range(3):
        entry = jnp.where(slot < count_ref[0], list_ref[0, slot], -2)
        allow = jnp.where(block == entry, 1.0, allow)
    marks[...] = allow.astype(bf16)
    stores = []
    for dest in range(8):
        stores.append(
            pltpu.make_async_copy(marks, out_ref.at[dest, 512:528], sems.at[4 + len(stores)])
        )
        stores[-1].start()
    for place, load in enumerate(loads):
        load.wait()
        targets = [out_ref.at[dest, place * 128 : place * 128 + 128] for dest in range(8)]
        if place == 0:
            targets += [twice_ref.at[0:128], twice_ref.at[128:256]]
        for target in targets:
            stores.append(
                pltpu.make_async_copy(held.at[place], target, sems.at[4 + len(stores)])
            )
            stores[-1].start()
    for store in stores:
        store.wait()


def pack_audio(where_ref, q_ref, g_ref, k_ref, v_ref, mine_ref, other_ref, wide):
    start = pl.multiple_of(where_ref[0] * 8, 8)
    core = lax.rem(where_ref[1], 2)
    for place, ref in enumerate((q_ref, g_ref, k_ref, v_ref)):
        wide[place, :, :] = ref[...].astype(f32)
    for shift in range(4):
        chip = lax.rem(where_ref[1] // 2 + shift, 4)
        for out, side in ((mine_ref, core), (other_ref, 1 - core)):
            cols = pl.ds(pl.multiple_of((chip * 2 + side) * 256, 256), 256)
            parts = [wide[place, pl.ds(start, 8), cols] for place in range(4)]
            out[shift, 0:16, :] = jnp.concatenate(parts[:2], 0).astype(bf16)
            out[shift, 16:32, :] = jnp.concatenate(parts[2:], 0).astype(bf16)


def pair_audio(mine_ref, other_ref, *outs):
    for shift in range(4):
        outs[shift][0] = mine_ref[shift]
        outs[shift][1] = other_ref[shift]


def gather_audio(where_ref, *rest):
    chunks, diag_ref, send_ref, wide_ref, flat_ref = rest[:4], *rest[4:]
    wide_ref[...] = jnp.zeros((4, 128, 256), f32)
    core = lax.rem(where_ref[1], 2)
    for piece in range(8):
        shift, side = piece // 2, piece % 2
        chip = lax.rem(where_ref[1] // 2 + (4 - shift), 4)
        source = chip * 2 + (core if side == 0 else 1 - core)
        part = chunks[shift][side].astype(f32)
        for place in range(4):
            piece_rows = part[place * 8 : place * 8 + 8, :]
            for h in range(2):
                rows = pl.ds(pl.multiple_of(source * 8 + h * 64, 8), 8)
                lanes = slice(h * 128, h * 128 + 128)
                wide_ref[place, rows, lanes] = piece_rows[:, lanes]
            if place >= 2:
                rows = pl.ds(pl.multiple_of(source * 8 + (place - 2) * 64, 8), 8)
                flat_ref[rows, :] = piece_rows
    diag_ref[...] = wide_ref[...].astype(bf16)
    flat = flat_ref[...].astype(bf16)
    for dest in range(8):
        send_ref[dest] = flat


def thirds(whole):
    high = whole.astype(bf16).astype(f32)
    middle = (whole - high).astype(bf16).astype(f32)
    return [high, middle, whole - high - middle]


def joined(rows):
    return rows[0:1, :] + rows[1:2, :] + rows[2:3, :]


def back_stats(packed_ref, diag_ref, stats_ref, score_ref, dprob_ref):
    queries, upstream = diag_ref[0], diag_ref[1]
    best = jnp.full((1, 128), -1e30, f32)
    for r in range(8):
        allowed = packed_ref[r, 512:528, 0:128].astype(f32)[0:1, :] > 0.5
        scores = dot_t(packed_ref[r, 128:256, :], queries) * SCALE
        score_ref[r] = scores
        dprob_ref[r] = dot_t(packed_ref[r, 256:384, :], upstream)
        peak = jnp.max(scores, axis=0, keepdims=True)
        best = jnp.maximum(best, jnp.where(allowed, peak, -1e30))
    total = jnp.zeros((1, 128), f32)
    delta = jnp.zeros((1, 128), f32)
    for r in range(8):
        allowed = packed_ref[r, 512:528, 0:128].astype(f32)[0:1, :] > 0.5
        weights = jnp.where(allowed, jnp.exp(score_ref[r] - best), 0.0)
        total += jnp.sum(weights, axis=0, keepdims=True)
        delta += jnp.sum(weights.astype(bf16).astype(f32) * dprob_ref[r], axis=0, keepdims=True)
    stats = thirds(best) + thirds(total) + thirds(delta) + [jnp.zeros((7, 128), f32)]
    stats = jnp.concatenate(stats, 0)
    stats_ref[...] = jnp.concatenate((stats, jnp.zeros((16, 128), f32)), 1).astype(bf16)


def self_part(cols_ref, packed_ref, stats_ref, out_ref):
    for block in range(8):
        logs = []
        for h in range(2):
            lanes = slice(h * 128, h * 128 + 128)
            queries = cols_ref[block, 0:128, lanes]
            keys = packed_ref[:, 128:256, lanes].reshape(1024, 128)
            values = packed_ref[:, 256:384, lanes].reshape(1024, 128)
            scores = dot_t(queries, keys)
            best = jnp.max(scores, axis=1, keepdims=True)
            weights = jnp.exp((scores - best) * SCALE)
            total = jnp.sum(weights, axis=1, keepdims=True)
            out = dot_n(weights.astype(bf16), values) / total
            out_ref[block, 0:128, lanes] = out.astype(bf16)
            logs.append(jnp.broadcast_to(best * SCALE + jnp.log(total), (128, 8)))
        whole = jnp.concatenate([jnp.transpose(part)[0:1, :] for part in logs], 1)
        rows = jnp.concatenate(thirds(whole) + [jnp.zeros((13, 256), f32)], 0)
        out_ref[block, 128:144, :] = rows.astype(bf16)
        out_ref[block, 144:160, :] = stats_ref[...]


def cross_part(where_ref, packed_ref, audio_ref, diag_ref, own_ref, gk_ref, gv_ref, out_ref):
    diag_key, diag_value = diag_ref[2], diag_ref[3]
    key_terms = jnp.zeros((128, 256), f32)
    value_terms = jnp.zeros((128, 256), f32)
    for r in range(8):
        allowed = packed_ref[r, 512:528, 0:128].astype(f32)[0:1, :] > 0.5
        queries2, upstream2 = packed_ref[r, 0:128, :], packed_ref[r, 384:512, :]
        stats = []
        for h in range(2):
            lanes = slice(h * 128, h * 128 + 128)
            keys = audio_ref[:, 0:64, lanes].reshape(512, 128)
            values = audio_ref[:, 64:128, lanes].reshape(512, 128)
            scores = dot_t(queries2[:, lanes], keys) * SCALE
            parts = [scores[:, b * 128 : b * 128 + 128] for b in range(4)]
            peak = jnp.where(allowed, functools.reduce(jnp.maximum, parts), -jnp.inf)
            best = jnp.max(peak, axis=1, keepdims=True)
            weights = [jnp.where(allowed, jnp.exp(p - best), 0.0) for p in parts]
            total = jnp.sum(sum(weights), axis=1, keepdims=True)
            weights = jnp.concatenate([w.astype(bf16) for w in weights], 1)
            out = dot_n(weights, values) / total
            out_ref[r, :, lanes] = out
            delta = jnp.sum(upstream2[:, lanes].astype(f32) * out, axis=1, keepdims=True)
            stats.append((best, total, delta))
        low_lanes = lax.broadcasted_iota(jnp.int32, (128, 128), 1) < 64
        best, total, delta = [jnp.where(low_lanes, s0, s1) for s0, s1 in zip(*stats)]
        scores = dot_t(queries2, diag_key) * SCALE
        probs = jnp.where(allowed, jnp.exp(scores - best), 0.0) / total
        dscores = probs * (dot_t(upstream2, diag_value) - delta)
        value_terms += dot_tn(probs.astype(bf16), upstream2)
        key_terms += dot_tn(dscores.astype(bf16), queries2)
    for h in range(2):
        rows, lanes = slice(h * 64, h * 64 + 64), slice(h * 128, h * 128 + 128)
        gk_ref[rows, :] = key_terms[rows, lanes] * SCALE
        gv_ref[rows, :] = value_terms[rows, lanes]
    own_ref[...] = out_ref[where_ref[0]]


def back_terms(sent_ref, packed_ref, diag_ref, gk_ref, gv_ref, out_ref):
    stats = [sent_ref[c, 144:160, 0:128].astype(f32) for c in range(8)]
    bests = [joined(part[0:3, :]) for part in stats]
    best = functools.reduce(jnp.maximum, bests)
    factors = [jnp.exp(part - best) for part in bests]
    total = sum(joined(part[3:6, :]) * factor for part, factor in zip(stats, factors))
    delta = sum(joined(part[6:9, :]) * factor for part, factor in zip(stats, factors)) / total
    queries, upstream = diag_ref[0], diag_ref[1]
    attn = jnp.zeros((128, 256), f32)
    grads = jnp.zeros((128, 256), f32)
    for r in range(8):
        allowed = packed_ref[r, 512:528, 0:128].astype(f32)[0:1, :] > 0.5
        keys, values = packed_ref[r, 128:256, :], packed_ref[r, 256:384, :]
        weights = jnp.where(allowed, jnp.exp(dot_t(keys, queries) * SCALE - best), 0.0)
        dscores = (weights / total) * (dot_t(values, upstream) - delta)
        attn += dot_tn(weights.astype(bf16), values)
        grads += dot_tn(dscores.astype(bf16), keys)
    totals = jnp.transpose(jnp.broadcast_to(total, (128, 128)))
    attn = jnp.concatenate((attn[:, 0:128] / totals, attn[:, 128:256] / totals), 1)
    grads = grads * SCALE
    for h in range(2):
        lanes = slice(h * 128, h * 128 + 128)
        for a in range(8):
            rows = slice(h * 64 + a * 8, h * 64 + a * 8 + 8)
            out_ref[a * 8 + h] = attn[rows, lanes]
            out_ref[a * 8 + 2 + h] = grads[rows, lanes]
            out_ref[a * 8 + 4 + h] = gk_ref[rows, :]
            out_ref[a * 8 + 6 + h] = gv_ref[rows, :]


def add_terms(terms_ref, out_ref):
    sums = [sum(terms_ref[a * 8 + c] for c in range(8)) for a in range(8)]
    sums = jnp.concatenate(sums, 0).astype(bf16)
    for dest in range(64):
        out_ref[dest] = sums


def lay_out(final_ref, *outs):
    for i in range(4):
        for h in range(2):
            for pair in range(4):
                first = final_ref[pair * 16 + i * 2 + h].astype(f32)
                second = final_ref[pair * 16 + 8 + i * 2 + h].astype(f32)
                for a in range(8):
                    both = jnp.concatenate(
                        (first[a * 8 : a * 8 + 8, :], second[a * 8 : a * 8 + 8, :]), 0
                    )
                    outs[i][
                        pair * 16 : pair * 16 + 16, a * 256 + h * 128 : a * 256 + h * 128 + 128
                    ] = both.astype(bf16)


def join_video(own_ref, sent_ref, out_ref):
    logs = [joined(sent_ref[c, 128:144, :].astype(f32)) for c in range(8)]
    best = functools.reduce(jnp.maximum, logs)
    shares = [jnp.exp(log - best) for log in logs]
    total = sum(shares)
    for h in range(2):
        lanes = slice(h * 128, h * 128 + 128)
        result = own_ref[:, lanes]
        for c in range(8):
            column = jnp.transpose(jnp.broadcast_to((shares[c] / total)[:, lanes], (128, 128)))
            result += sent_ref[c, 0:128, lanes].astype(f32) * column
        out_ref[:, lanes] = result.astype(bf16)


def rotate(value, axis, shift):
    count = lax.axis_size(axis)
    return lax.ppermute(value, axis, [(i, (i + shift) % count) for i in range(count)])


def local(
    video_query,
    video_key,
    video_value,
    audio_query,
    audio_key,
    audio_value,
    video_grad,
    audio_grad,
    block_list,
    block_count,
):
    where = jnp.stack(
        (lax.axis_index(ROWS), lax.axis_index(AUD), lax.axis_index(COLS))
    ).astype(jnp.int32)

    mine, other = call(
        pack_audio,
        [((4, CHUNK, 256), bf16)] * 2,
        10**6,
        scratch=[pltpu.VMEM((4, 64, 2048), f32)],
        smem=1,
        args=(where, audio_query, audio_grad, audio_key, audio_value),
    )
    other = rotate(other, "core", 1)
    packed, twice = call(
        pack_video,
        [((8, PACK, 256), bf16), ((256, 256), bf16)],
        10**6,
        scratch=[
            pltpu.VMEM((4, 128, 256), bf16),
            pltpu.VMEM((16, 256), bf16),
            pltpu.SemaphoreType.DMA((46,)),
        ],
        in_specs=[SM, SM] + [HBM] * 4,
        limit=60 * 1024 * 1024,
        out_specs=[HBM, HBM],
        args=(block_list, block_count, video_query, video_key, video_value, video_grad),
    )
    cols_query = lax.all_gather(twice, COLS)
    packed = lax.all_to_all(packed, ROWS, 0, 0, tiled=True)
    chunks = call(pair_audio, [((2, CHUNK, 256), bf16)] * 4, 10**6, args=(mine, other))
    chunks = [chunks[0]] + [rotate(chunks[shift], "yh", shift) for shift in range(1, 4)]

    diag, shared = call(
        gather_audio,
        [((4, 128, 256), bf16), ((8, 128, 256), bf16)],
        10**6,
        scratch=[pltpu.VMEM((4, 128, 256), f32), pltpu.VMEM((128, 256), f32)],
        smem=1,
        args=(where, *chunks),
    )
    packed, shared = lax.optimization_barrier((packed, shared))
    shared = lax.all_to_all(shared, ROWS, 0, 0, tiled=True)
    (stats,) = call(
        back_stats,
        [((16, 256), bf16)],
        10**9,
        scratch=[pltpu.VMEM((8, 128, 128), f32)] * 2,
        args=(packed, diag),
    )
    (sent,) = call(
        self_part, [((8, SENT, 256), bf16)], 4 * 10**9, args=(cols_query, packed, stats)
    )
    sent, shared = lax.optimization_barrier((sent, shared))
    sent = lax.all_to_all(sent, COLS, 0, 0, tiled=True)
    cross_own, key_terms, value_terms = call(
        cross_part,
        [((128, 256), f32), ((128, 128), f32), ((128, 128), f32)],
        4 * 10**9,
        scratch=[pltpu.VMEM((8, 128, 256), f32)],
        smem=1,
        args=(where, packed, shared, diag),
    )
    (terms,) = call(
        back_terms,
        [((64, 8, 128), f32)],
        10**9,
        args=(sent, packed, diag, key_terms, value_terms),
    )
    terms = lax.all_to_all(terms, AUD + COLS, 0, 0, tiled=True)
    (video_out,) = call(join_video, [((128, 256), bf16)], 10**7, args=(cross_own, sent))
    (summed,) = call(add_terms, [((64, 64, 128), bf16)], 10**6, args=(terms,))
    final = lax.all_to_all(summed, SEQ, 0, 0, tiled=True)
    finished = call(lay_out, [((64, 2048), bf16)] * 4, 10**6, args=(final,))
    return (video_out, *finished)


def solution(mesh):
    fine = Mesh(mesh.devices.reshape(4, 2, 8, 4, 2), ("x", "yl", "z", "yh", "core"))
    video, audio = P(SEQ, AUD), P(AUD, None)
    return jax.shard_map(
        local,
        mesh=fine,
        in_specs=(
            video,
            video,
            video,
            audio,
            audio,
            audio,
            video,
            audio,
            P(SEQ, None),
            P(SEQ),
        ),
        out_specs=(video, audio, audio, audio, audio),
        check_vma=False,
    )
```

```python
import functools
import math

import jax
import jax.numpy as jnp
from jax import lax
from jax.experimental import pallas as pl
from jax.experimental.pallas import tpu as pltpu
from jax.sharding import Mesh, PartitionSpec as P

HEAD_DIM = 128
ROWS = ("x", "yl")
COLS = ("z",)
AUD = ("yh", "core")
SEQ = ROWS + COLS
SCALE = 1.0 / math.sqrt(HEAD_DIM)
bf16 = jnp.bfloat16
f32 = jnp.float32
VMEM_LIMIT = 20 * 1024 * 1024
PACK = 656
CHUNK = 32
SENT = 144


VM = pl.BlockSpec(memory_space=pltpu.VMEM)
SM = pl.BlockSpec(memory_space=pltpu.SMEM)
HBM = pl.BlockSpec(memory_space=pl.ANY)


def call(
    kernel,
    outs,
    flops,
    scratch=(),
    smem=0,
    args=(),
    in_specs=None,
    out_specs=None,
    limit=VMEM_LIMIT,
    aliases=None,
):
    return pl.pallas_call(
        kernel,
        out_shape=[jax.ShapeDtypeStruct(s, d) for s, d in outs],
        in_specs=in_specs or [SM] * smem + [VM] * (len(args) - smem),
        out_specs=out_specs or [VM] * len(outs),
        scratch_shapes=list(scratch),
        input_output_aliases=aliases or {},
        compiler_params=pltpu.CompilerParams(vmem_limit_bytes=limit),
        cost_estimate=pl.CostEstimate(flops=flops, bytes_accessed=4000000, transcendentals=0),
    )(*args)


def dot_t(left, right):
    return lax.dot_general(left, right, (((1,), (1,)), ((), ())), preferred_element_type=f32)


def dot_n(left, right):
    return lax.dot_general(left, right, (((1,), (0,)), ((), ())), preferred_element_type=f32)


def dot_tn(left, right):
    return lax.dot_general(left, right, (((0,), (0,)), ((), ())), preferred_element_type=f32)


def side_by_side(first_ref, second_ref, out_ref):
    count = first_ref.shape[0]
    out_ref[0:count] = first_ref[...]
    out_ref[count : 2 * count] = second_ref[...]


def pack_video(list_ref, count_ref, *rest):
    ins, out_ref, held, marks, sems = rest[:4], *rest[4:]
    loads = [
        pltpu.make_async_copy(ref, held.at[place], sems.at[place])
        for place, ref in enumerate(ins)
    ]
    for load in loads:
        load.start()
    lanes = lax.broadcasted_iota(jnp.int32, (16, 256), 1)
    block = (lanes % 64) // 16
    allow = jnp.zeros((16, 256), f32)
    for slot in range(3):
        entry = jnp.where(slot < count_ref[0], list_ref[0, slot], -2)
        allow = jnp.where(block == entry, 1.0, allow)
    marks[...] = allow.astype(bf16)
    stores = []
    for dest in range(8):
        stores.append(
            pltpu.make_async_copy(marks, out_ref.at[dest, 512:528], sems.at[4 + len(stores)])
        )
        stores[-1].start()
    for place, load in enumerate(loads):
        load.wait()
        for dest in range(8):
            target = out_ref.at[dest, place * 128 : place * 128 + 128]
            stores.append(
                pltpu.make_async_copy(held.at[place], target, sems.at[4 + len(stores)])
            )
            stores[-1].start()
    for store in stores:
        store.wait()


def pack_audio(*rest):
    ins, out_ref, held, sems = rest[:4], *rest[4:]
    row = lax.axis_index(ROWS)
    pair = pl.ds(pl.multiple_of(row // 2 * 16, 16), 16)
    loads = [
        pltpu.make_async_copy(ref.at[pair], held.at[place], sems.at[place])
        for place, ref in enumerate(ins)
    ]
    for load in loads:
        load.start()
    parts = []
    for place, load in enumerate(loads):
        load.wait()
        both = held[place].astype(f32)
        parts.append(jnp.where(lax.rem(row, 2) == 0, both[0:8, :], both[8:16, :]))
    parts = jnp.concatenate(parts, 0).astype(bf16)
    for dest in range(8):
        out_ref[dest] = parts[:, dest * 256 : dest * 256 + 256]


def add_audio(audio_ref, given_ref, diag_ref, out_ref, wide_ref, flat_ref, flat16_ref, sems):
    for source in range(8):
        part = audio_ref[source].astype(f32)
        for place in (2, 3):
            row = source * 8 + (place - 2) * 64
            flat_ref[row : row + 8, :] = part[place * 8 : place * 8 + 8, :]
    flat16_ref[...] = flat_ref[...].astype(bf16)
    stores = [
        pltpu.make_async_copy(flat16_ref, out_ref.at[dest, 528:656], sems.at[dest])
        for dest in range(8)
    ]
    for store in stores:
        store.start()
    wide_ref[...] = jnp.zeros((4, 128, 256), f32)
    for source in range(8):
        part = audio_ref[source].astype(f32)
        for place in range(4):
            for h in range(2):
                row, lanes = source * 8 + h * 64, slice(h * 128, h * 128 + 128)
                wide_ref[place, row : row + 8, lanes] = part[place * 8 : place * 8 + 8, lanes]
    diag_ref[...] = wide_ref[...].astype(bf16)
    for store in stores:
        store.wait()


def thirds(whole):
    high = whole.astype(bf16).astype(f32)
    middle = (whole - high).astype(bf16).astype(f32)
    return [high, middle, whole - high - middle]


def joined(rows):
    return rows[0:1, :] + rows[1:2, :] + rows[2:3, :]


def back_stats(packed_ref, diag_ref, stats_ref, score_ref, dprob_ref):
    queries, upstream = diag_ref[0], diag_ref[1]
    best = jnp.full((1, 128), -1e30, f32)
    for r in range(8):
        allowed = packed_ref[r, 512:528, 0:128].astype(f32)[0:1, :] > 0.5
        scores = dot_t(packed_ref[r, 128:256, :], queries) * SCALE
        score_ref[r] = scores
        dprob_ref[r] = dot_t(packed_ref[r, 256:384, :], upstream)
        peak = jnp.max(scores, axis=0, keepdims=True)
        best = jnp.maximum(best, jnp.where(allowed, peak, -1e30))
    total = jnp.zeros((1, 128), f32)
    delta = jnp.zeros((1, 128), f32)
    for r in range(8):
        allowed = packed_ref[r, 512:528, 0:128].astype(f32)[0:1, :] > 0.5
        weights = jnp.where(allowed, jnp.exp(score_ref[r] - best), 0.0)
        total += jnp.sum(weights, axis=0, keepdims=True)
        delta += jnp.sum(weights.astype(bf16).astype(f32) * dprob_ref[r], axis=0, keepdims=True)
    stats = thirds(best) + thirds(total) + thirds(delta) + [jnp.zeros((4, 128), f32)]
    stats = jnp.concatenate(stats, 0)
    stats_ref[...] = jnp.concatenate((stats, jnp.zeros((13, 128), f32)), 1)


def self_part(near_ref, far_ref, packed_ref, stats_ref, out_ref):
    column = lax.axis_index("z")
    for part_ref, distances in ((near_ref, (0, 4, 2, 6)), (far_ref, (1, 5, 3, 7))):
        logs = []
        for h in range(2):
            lanes = slice(h * 128, h * 128 + 128)
            queries = part_ref[:, :, lanes].reshape(512, 128)
            keys = packed_ref[:, 128:256, lanes].reshape(1024, 128)
            values = packed_ref[:, 256:384, lanes].reshape(1024, 128)
            scores = dot_t(queries, keys)
            best = jnp.max(scores, axis=1, keepdims=True)
            weights = jnp.exp2((scores - best) * (SCALE * math.log2(math.e)))
            total = jnp.sum(weights, axis=1, keepdims=True)
            out = dot_n(weights.astype(bf16), values) / total
            out = out.astype(bf16).reshape(4, 128, 128)
            for place, distance in enumerate(distances):
                out_ref[7 - (column ^ distance), 0:128, lanes] = out[place]
            logs.append(jnp.broadcast_to(best * SCALE + jnp.log(total), (512, 128)))
        logs = [jnp.transpose(part)[0:1, :] for part in logs]
        for place, distance in enumerate(distances):
            whole = jnp.concatenate([part[:, place * 128 : place * 128 + 128] for part in logs], 1)
            rows = jnp.concatenate(thirds(whole) + [stats_ref[...]], 0)
            out_ref[7 - (column ^ distance), 128:144, :] = rows.astype(bf16)


def cross_part(
    packed_ref, diag_ref, own_ref, sums_ref, out_ref
):
    diag_key, diag_value = diag_ref[2], diag_ref[3]
    key_terms = jnp.zeros((128, 256), f32)
    value_terms = jnp.zeros((128, 256), f32)
    for r in range(8):
        allowed = packed_ref[r, 512:528, 0:128].astype(f32)[0:1, :] > 0.5
        queries2, upstream2 = packed_ref[r, 0:128, :], packed_ref[r, 384:512, :]
        stats = []
        for h in range(2):
            lanes = slice(h * 128, h * 128 + 128)
            keys = packed_ref[:, 528:592, lanes].reshape(512, 128)
            values = packed_ref[:, 592:656, lanes].reshape(512, 128)
            scores = dot_t(queries2[:, lanes], keys) * SCALE
            parts = [scores[:, b * 128 : b * 128 + 128] for b in range(4)]
            peak = jnp.where(allowed, functools.reduce(jnp.maximum, parts), -jnp.inf)
            best = jnp.max(peak, axis=1, keepdims=True)
            weights = [jnp.where(allowed, jnp.exp(p - best), 0.0) for p in parts]
            total = jnp.sum(sum(weights), axis=1, keepdims=True)
            weights = jnp.concatenate([w.astype(bf16) for w in weights], 1)
            out = dot_n(weights, values) / total
            out_ref[r, :, lanes] = out
            delta = jnp.sum(upstream2[:, lanes].astype(f32) * out, axis=1, keepdims=True)
            stats.append((best, total, delta))
        low_lanes = lax.broadcasted_iota(jnp.int32, (128, 128), 1) < 64
        best, total, delta = [jnp.where(low_lanes, s0, s1) for s0, s1 in zip(*stats)]
        scores = dot_t(queries2, diag_key) * SCALE
        probs = jnp.where(allowed, jnp.exp(scores - best), 0.0) / total
        dscores = probs * (dot_t(upstream2, diag_value) - delta)
        value_terms += dot_tn(probs.astype(bf16), upstream2)
        key_terms += dot_tn(dscores.astype(bf16), queries2)
    for h in range(2):
        rows, lanes = slice(h * 64, h * 64 + 64), slice(h * 128, h * 128 + 128)
        sums_ref[0, rows, :] = key_terms[rows, lanes] * SCALE
        sums_ref[1, rows, :] = value_terms[rows, lanes]
    own_ref[...] = out_ref[lax.axis_index(ROWS)]


def back_terms(
    sent_ref, packed_ref, diag_far_ref, sums_far_ref, out_ref, diag_ref, sums_ref, sems
):
    loads = [
        pltpu.make_async_copy(diag_far_ref.at[0:2], diag_ref, sems.at[0]),
        pltpu.make_async_copy(sums_far_ref, sums_ref, sems.at[1]),
    ]
    for load in loads:
        load.start()
    stats = [sent_ref[c, 128:144, 0:128].astype(f32) for c in range(8)]
    bests = [joined(part[3:6, :]) for part in stats]
    best = functools.reduce(jnp.maximum, bests)
    factors = [jnp.exp(part - best) for part in bests]
    total = sum(joined(part[6:9, :]) * factor for part, factor in zip(stats, factors))
    delta = sum(joined(part[9:12, :]) * factor for part, factor in zip(stats, factors)) / total
    for load in loads:
        load.wait()
    queries, upstream = diag_ref[0], diag_ref[1]
    attn = jnp.zeros((128, 256), f32)
    grads = jnp.zeros((128, 256), f32)
    for r in range(8):
        allowed = packed_ref[r, 512:528, 0:128].astype(f32)[0:1, :] > 0.5
        keys, values = packed_ref[r, 128:256, :], packed_ref[r, 256:384, :]
        weights = jnp.where(allowed, jnp.exp(dot_t(keys, queries) * SCALE - best), 0.0)
        dscores = (weights / total) * (dot_t(values, upstream) - delta)
        attn += dot_tn(weights.astype(bf16), values)
        grads += dot_tn(dscores.astype(bf16), keys)
    totals = jnp.transpose(jnp.broadcast_to(total, (128, 128)))
    attn = jnp.concatenate((attn[:, 0:128] / totals, attn[:, 128:256] / totals), 1)
    grads = grads * SCALE
    for h in range(2):
        lanes = slice(h * 128, h * 128 + 128)
        for a in range(8):
            rows = slice(h * 64 + a * 8, h * 64 + a * 8 + 8)
            out_ref[a * 8 + h] = attn[rows, lanes]
            out_ref[a * 8 + 2 + h] = grads[rows, lanes]
            out_ref[a * 8 + 4 + h] = sums_ref[0, rows, :]
            out_ref[a * 8 + 6 + h] = sums_ref[1, rows, :]


def add_terms(terms_ref, out_ref):
    sums = [sum(terms_ref[a * 8 + c] for c in range(8)) for a in range(8)]
    sums = jnp.concatenate(sums, 0).astype(bf16)
    for dest in range(8):
        out_ref[dest] = sums


def again(ref, out_ref):
    for dest in range(8):
        out_ref[dest] = ref[...]


def lay_out(final_ref, *outs):
    for i in range(4):
        for h in range(2):
            for pair in range(4):
                first = final_ref[pair * 2, 7 - i * 2 - h].astype(f32)
                second = final_ref[pair * 2 + 1, 7 - i * 2 - h].astype(f32)
                for a in range(8):
                    both = jnp.concatenate(
                        (first[a * 8 : a * 8 + 8, :], second[a * 8 : a * 8 + 8, :]), 0
                    )
                    outs[i][
                        pair * 16 : pair * 16 + 16, a * 256 + h * 128 : a * 256 + h * 128 + 128
                    ] = both.astype(bf16)


def join_video(own_ref, sent_ref, out_ref):
    logs = [joined(sent_ref[c, 128:144, :].astype(f32)) for c in range(8)]
    best = functools.reduce(jnp.maximum, logs)
    shares = [jnp.exp(log - best) for log in logs]
    total = sum(shares)
    for h in range(2):
        lanes = slice(h * 128, h * 128 + 128)
        result = own_ref[:, lanes]
        for c in range(8):
            column = jnp.transpose(jnp.broadcast_to((shares[c] / total)[:, lanes], (128, 128)))
            result += sent_ref[c, 0:128, lanes].astype(f32) * column
        out_ref[:, lanes] = result.astype(bf16)


def swap(value, axis, distance):
    count = lax.axis_size(axis)
    return lax.ppermute(value, axis, [(i, i ^ distance) for i in range(count)])


def backwards(value):
    return lax.all_to_all(
        value, "z", 0, 0, axis_index_groups=[[7, 6, 5, 4, 3, 2, 1, 0]], tiled=True
    )


def local(
    video_query,
    video_key,
    video_value,
    audio_query,
    audio_key,
    audio_value,
    video_grad,
    audio_grad,
    block_list,
    block_count,
):
    (audio,) = call(
        pack_audio,
        [((8, CHUNK, 256), bf16)],
        10**6,
        scratch=[
            pltpu.VMEM((4, 16, 2048), bf16),
            pltpu.SemaphoreType.DMA((4,)),
        ],
        in_specs=[HBM] * 4,
        limit=60 * 1024 * 1024,
        args=(audio_query, audio_grad, audio_key, audio_value),
    )
    audio = lax.all_to_all(audio, AUD, 0, 0, tiled=True)
    (packed,) = call(
        pack_video,
        [((8, PACK, 256), bf16)],
        10**6,
        scratch=[
            pltpu.VMEM((4, 128, 256), bf16),
            pltpu.VMEM((16, 256), bf16),
            pltpu.SemaphoreType.DMA((44,)),
        ],
        in_specs=[SM, SM] + [HBM] * 4,
        out_specs=[HBM],
        limit=60 * 1024 * 1024,
        args=(block_list, block_count, video_query, video_key, video_value, video_grad),
    )
    diag, packed = call(
        add_audio,
        [((4, 128, 256), bf16), ((8, PACK, 256), bf16)],
        10**6,
        scratch=[
            pltpu.VMEM((4, 128, 256), f32),
            pltpu.VMEM((128, 256), f32),
            pltpu.VMEM((128, 256), bf16),
            pltpu.SemaphoreType.DMA((8,)),
        ],
        in_specs=[VM, HBM],
        out_specs=[VM, HBM],
        aliases={1: 1},
        limit=60 * 1024 * 1024,
        args=(audio, packed),
    )
    near = video_query.reshape(1, 128, 256)
    packed, near = lax.optimization_barrier((packed, near))
    packed = lax.all_to_all(packed, ROWS, 0, 0, tiled=True)
    for distance in (4, 2):
        far = swap(near, "z", distance)
        (near,) = call(
            side_by_side, [((2 * near.shape[0], 128, 256), bf16)], 10**6, args=(near, far)
        )
    far = swap(near, "z", 1)
    (stats,) = call(
        back_stats,
        [((13, 256), f32)],
        10**9,
        scratch=[pltpu.VMEM((8, 128, 128), f32)] * 2,
        args=(packed, diag),
    )
    (sent,) = call(
        self_part,
        [((8, SENT, 256), bf16)],
        4 * 10**9,
        args=(near, far, packed, stats),
    )
    sent = backwards(sent)
    cross_own, sums = call(
        cross_part,
        [((128, 256), f32), ((2, 128, 128), f32)],
        4 * 10**9,
        scratch=[pltpu.VMEM((8, 128, 256), f32)],
        args=(packed, diag),
    )
    (terms,) = call(
        back_terms,
        [((64, 8, 128), f32)],
        10**9,
        scratch=[
            pltpu.VMEM((2, 128, 256), bf16),
            pltpu.VMEM((2, 128, 128), f32),
            pltpu.SemaphoreType.DMA((2,)),
        ],
        in_specs=[VM, VM, HBM, HBM],
        limit=48 * 1024 * 1024,
        args=(sent, packed, diag, sums),
    )
    terms = lax.all_to_all(terms, AUD + COLS, 0, 0, tiled=True)
    (video_out,) = call(join_video, [((128, 256), bf16)], 10**7, args=(cross_own, sent))
    (summed,) = call(add_terms, [((8, 64, 128), bf16)], 10**6, args=(terms,))
    final = backwards(summed)
    (final,) = call(again, [((8, 8, 64, 128), bf16)], 10**6, args=(final,))
    final = lax.all_to_all(final, ROWS, 0, 0, tiled=True)
    finished = call(lay_out, [((64, 2048), bf16)] * 4, 10**6, args=(final,))
    return (video_out, *finished)


def solution(mesh):
    fine = Mesh(mesh.devices.reshape(4, 2, 8, 4, 2), ("x", "yl", "z", "yh", "core"))
    video, audio = P(SEQ, AUD), P(AUD, None)
    return jax.shard_map(
        local,
        mesh=fine,
        in_specs=(
            video,
            video,
            video,
            audio,
            audio,
            audio,
            video,
            audio,
            P(SEQ, None),
            P(SEQ),
        ),
        out_specs=(video, audio, audio, audio, audio),
        check_vma=False,
    )
```

```python
import functools
import math

import jax
import jax.numpy as jnp
from jax import lax
from jax.experimental import pallas as pl
from jax.experimental.pallas import tpu as pltpu
from jax.sharding import Mesh, PartitionSpec as P

HEAD_DIM = 128
ROWS = ("x", "yl")
COLS = ("z",)
AUD = ("yh", "core")
SEQ = ROWS + COLS
SCALE = 1.0 / math.sqrt(HEAD_DIM)
bf16 = jnp.bfloat16
f32 = jnp.float32
VMEM_LIMIT = 20 * 1024 * 1024
PACK = 656
CHUNK = 32
SENT = 144


VM = pl.BlockSpec(memory_space=pltpu.VMEM)
SM = pl.BlockSpec(memory_space=pltpu.SMEM)
HBM = pl.BlockSpec(memory_space=pl.ANY)


def call(
    kernel,
    outs,
    flops,
    scratch=(),
    smem=0,
    args=(),
    in_specs=None,
    out_specs=None,
    limit=VMEM_LIMIT,
    aliases=None,
):
    return pl.pallas_call(
        kernel,
        out_shape=[jax.ShapeDtypeStruct(s, d) for s, d in outs],
        in_specs=in_specs or [SM] * smem + [VM] * (len(args) - smem),
        out_specs=out_specs or [VM] * len(outs),
        scratch_shapes=list(scratch),
        input_output_aliases=aliases or {},
        compiler_params=pltpu.CompilerParams(vmem_limit_bytes=limit),
        cost_estimate=pl.CostEstimate(flops=flops, bytes_accessed=4000000, transcendentals=0),
    )(*args)


def dot_t(left, right):
    return lax.dot_general(left, right, (((1,), (1,)), ((), ())), preferred_element_type=f32)


def dot_n(left, right):
    return lax.dot_general(left, right, (((1,), (0,)), ((), ())), preferred_element_type=f32)


def dot_tn(left, right):
    return lax.dot_general(left, right, (((0,), (0,)), ((), ())), preferred_element_type=f32)


def side_by_side(first_ref, second_ref, out_ref):
    count = first_ref.shape[0]
    out_ref[0:count] = first_ref[...]
    out_ref[count : 2 * count] = second_ref[...]


def pack_video(list_ref, count_ref, *rest):
    ins, out_ref, held, marks, sems = rest[:4], *rest[4:]
    loads = [
        pltpu.make_async_copy(ref, held.at[place], sems.at[place])
        for place, ref in enumerate(ins)
    ]
    for load in loads:
        load.start()
    lanes = lax.broadcasted_iota(jnp.int32, (16, 256), 1)
    block = (lanes % 64) // 16
    allow = jnp.zeros((16, 256), f32)
    for slot in range(3):
        entry = jnp.where(slot < count_ref[0], list_ref[0, slot], -2)
        allow = jnp.where(block == entry, 1.0, allow)
    marks[...] = allow.astype(bf16)
    stores = []
    for dest in range(8):
        stores.append(
            pltpu.make_async_copy(marks, out_ref.at[dest, 32], sems.at[4 + len(stores)])
        )
        stores[-1].start()
    for place, load in enumerate(loads):
        load.wait()
        for dest in range(8):
            target = out_ref.at[dest, place * 8 : place * 8 + 8]
            stores.append(
                pltpu.make_async_copy(held.at[place], target, sems.at[4 + len(stores)])
            )
            stores[-1].start()
    for store in stores:
        store.wait()


def pack_audio(*rest):
    ins, out_ref, held, sems = rest[:4], *rest[4:]
    row = lax.axis_index(ROWS)
    pair = pl.ds(pl.multiple_of(row // 2 * 16, 16), 16)
    loads = [
        pltpu.make_async_copy(ref.at[pair], held.at[place], sems.at[place])
        for place, ref in enumerate(ins)
    ]
    for load in loads:
        load.start()
    parts = []
    for place, load in enumerate(loads):
        load.wait()
        both = held[place].astype(f32)
        parts.append(jnp.where(lax.rem(row, 2) == 0, both[0:8, :], both[8:16, :]))
    parts = jnp.concatenate(parts, 0).astype(bf16)
    for dest in range(8):
        out_ref[dest] = parts[:, dest * 256 : dest * 256 + 256]


def add_audio(audio_ref, given_ref, diag_ref, out_ref, wide_ref, sems):
    stores = [
        pltpu.make_async_copy(audio_ref.at[:, 16:32], out_ref.at[dest, 33:41], sems.at[dest])
        for dest in range(8)
    ]
    for store in stores:
        store.start()
    wide_ref[...] = jnp.zeros((4, 128, 256), f32)
    for source in range(8):
        part = audio_ref[source].astype(f32)
        for place in range(4):
            for h in range(2):
                row, lanes = source * 8 + h * 64, slice(h * 128, h * 128 + 128)
                wide_ref[place, row : row + 8, lanes] = part[place * 8 : place * 8 + 8, lanes]
    diag_ref[...] = wide_ref[...].astype(bf16)
    for store in stores:
        store.wait()


def thirds(whole):
    high = whole.astype(bf16).astype(f32)
    middle = (whole - high).astype(bf16).astype(f32)
    return [high, middle, whole - high - middle]


def joined(rows):
    return rows[0:1, :] + rows[1:2, :] + rows[2:3, :]


def back_stats(packed_ref, diag_ref, stats_ref, score_ref, dprob_ref):
    queries, upstream = diag_ref[0], diag_ref[1]
    best = jnp.full((1, 128), -1e30, f32)
    for r in range(8):
        allowed = packed_ref[r, 512:528, 0:128].astype(f32)[0:1, :] > 0.5
        scores = dot_t(packed_ref[r, 128:256, :], queries) * SCALE
        score_ref[r] = scores
        dprob_ref[r] = dot_t(packed_ref[r, 256:384, :], upstream)
        peak = jnp.max(scores, axis=0, keepdims=True)
        best = jnp.maximum(best, jnp.where(allowed, peak, -1e30))
    total = jnp.zeros((1, 128), f32)
    delta = jnp.zeros((1, 128), f32)
    for r in range(8):
        allowed = packed_ref[r, 512:528, 0:128].astype(f32)[0:1, :] > 0.5
        weights = jnp.where(allowed, jnp.exp(score_ref[r] - best), 0.0)
        total += jnp.sum(weights, axis=0, keepdims=True)
        delta += jnp.sum(weights.astype(bf16).astype(f32) * dprob_ref[r], axis=0, keepdims=True)
    stats = thirds(best) + thirds(total) + thirds(delta) + [jnp.zeros((4, 128), f32)]
    stats = jnp.concatenate(stats, 0)
    stats_ref[...] = jnp.concatenate((stats, jnp.zeros((13, 128), f32)), 1)


def self_part(near_ref, far_ref, packed_ref, stats_ref, out_ref):
    column = lax.axis_index("z")
    for part_ref, distances in ((near_ref, (0, 4, 2, 6)), (far_ref, (1, 5, 3, 7))):
        logs = []
        for h in range(2):
            lanes = slice(h * 128, h * 128 + 128)
            queries = part_ref[:, :, lanes].reshape(512, 128)
            keys = packed_ref[:, 128:256, lanes].reshape(1024, 128)
            values = packed_ref[:, 256:384, lanes].reshape(1024, 128)
            scores = dot_t(queries, keys)
            best = jnp.max(scores, axis=1, keepdims=True)
            weights = jnp.exp2((scores - best) * (SCALE * math.log2(math.e)))
            total = jnp.sum(weights, axis=1, keepdims=True)
            out = dot_n(weights.astype(bf16), values) / total
            out = out.astype(bf16).reshape(4, 128, 128)
            for place, distance in enumerate(distances):
                out_ref[7 - (column ^ distance), 0:128, lanes] = out[place]
            logs.append(jnp.broadcast_to(best * SCALE + jnp.log(total), (512, 128)))
        logs = [jnp.transpose(part)[0:1, :] for part in logs]
        for place, distance in enumerate(distances):
            whole = jnp.concatenate([part[:, place * 128 : place * 128 + 128] for part in logs], 1)
            rows = jnp.concatenate(thirds(whole) + [stats_ref[...]], 0)
            out_ref[7 - (column ^ distance), 128:144, :] = rows.astype(bf16)


def cross_part(
    packed_ref, diag_ref, own_ref, sums_ref, out_ref
):
    diag_key, diag_value = diag_ref[2], diag_ref[3]
    audio = packed_ref[:, 528:656, :].astype(f32).reshape(8, 8, 16, 256)
    all_keys = audio[:, :, 0:8, :].reshape(512, 256).astype(bf16)
    all_values = audio[:, :, 8:16, :].reshape(512, 256).astype(bf16)
    key_terms = jnp.zeros((128, 256), f32)
    value_terms = jnp.zeros((128, 256), f32)
    for r in range(8):
        allowed = packed_ref[r, 512:528, 0:128].astype(f32)[0:1, :] > 0.5
        queries2, upstream2 = packed_ref[r, 0:128, :], packed_ref[r, 384:512, :]
        stats = []
        for h in range(2):
            lanes = slice(h * 128, h * 128 + 128)
            scores = dot_t(queries2[:, lanes], all_keys[:, lanes]) * SCALE
            parts = [scores[:, b * 128 : b * 128 + 128] for b in range(4)]
            peak = jnp.where(allowed, functools.reduce(jnp.maximum, parts), -jnp.inf)
            best = jnp.max(peak, axis=1, keepdims=True)
            weights = [jnp.where(allowed, jnp.exp(p - best), 0.0) for p in parts]
            total = jnp.sum(sum(weights), axis=1, keepdims=True)
            weights = jnp.concatenate([w.astype(bf16) for w in weights], 1)
            out = dot_n(weights, all_values[:, lanes]) / total
            out_ref[r, :, lanes] = out
            delta = jnp.sum(upstream2[:, lanes].astype(f32) * out, axis=1, keepdims=True)
            stats.append((best, total, delta))
        low_lanes = lax.broadcasted_iota(jnp.int32, (128, 128), 1) < 64
        best, total, delta = [jnp.where(low_lanes, s0, s1) for s0, s1 in zip(*stats)]
        scores = dot_t(queries2, diag_key) * SCALE
        probs = jnp.where(allowed, jnp.exp(scores - best), 0.0) / total
        dscores = probs * (dot_t(upstream2, diag_value) - delta)
        value_terms += dot_tn(probs.astype(bf16), upstream2)
        key_terms += dot_tn(dscores.astype(bf16), queries2)
    for h in range(2):
        rows, lanes = slice(h * 64, h * 64 + 64), slice(h * 128, h * 128 + 128)
        sums_ref[0, rows, :] = key_terms[rows, lanes] * SCALE
        sums_ref[1, rows, :] = value_terms[rows, lanes]
    own_ref[...] = out_ref[lax.axis_index(ROWS)]


def back_terms(
    sent_ref, packed_ref, diag_far_ref, sums_far_ref, out_ref, diag_ref, sums_ref, sems
):
    loads = [
        pltpu.make_async_copy(diag_far_ref.at[0:2], diag_ref, sems.at[0]),
        pltpu.make_async_copy(sums_far_ref, sums_ref, sems.at[1]),
    ]
    for load in loads:
        load.start()
    stats = [sent_ref[c, 128:144, 0:128].astype(f32) for c in range(8)]
    bests = [joined(part[3:6, :]) for part in stats]
    best = functools.reduce(jnp.maximum, bests)
    factors = [jnp.exp(part - best) for part in bests]
    total = sum(joined(part[6:9, :]) * factor for part, factor in zip(stats, factors))
    delta = sum(joined(part[9:12, :]) * factor for part, factor in zip(stats, factors)) / total
    for load in loads:
        load.wait()
    queries, upstream = diag_ref[0], diag_ref[1]
    attn = jnp.zeros((128, 256), f32)
    grads = jnp.zeros((128, 256), f32)
    for r in range(8):
        allowed = packed_ref[r, 512:528, 0:128].astype(f32)[0:1, :] > 0.5
        keys, values = packed_ref[r, 128:256, :], packed_ref[r, 256:384, :]
        weights = jnp.where(allowed, jnp.exp(dot_t(keys, queries) * SCALE - best), 0.0)
        dscores = (weights / total) * (dot_t(values, upstream) - delta)
        attn += dot_tn(weights.astype(bf16), values)
        grads += dot_tn(dscores.astype(bf16), keys)
    totals = jnp.transpose(jnp.broadcast_to(total, (128, 128)))
    attn = jnp.concatenate((attn[:, 0:128] / totals, attn[:, 128:256] / totals), 1)
    grads = grads * SCALE
    for h in range(2):
        lanes = slice(h * 128, h * 128 + 128)
        for a in range(8):
            rows = slice(h * 64 + a * 8, h * 64 + a * 8 + 8)
            out_ref[63 - (a * 8 + h)] = attn[rows, lanes]
            out_ref[63 - (a * 8 + 2 + h)] = grads[rows, lanes]
            out_ref[63 - (a * 8 + 4 + h)] = sums_ref[0, rows, :]
            out_ref[63 - (a * 8 + 6 + h)] = sums_ref[1, rows, :]


def add_terms(terms_ref, out_ref):
    sums = [sum(terms_ref[(7 - a) * 8 + c] for c in range(8)) for a in range(8)]
    sums = jnp.concatenate(sums, 0).astype(bf16)
    for dest in range(8):
        out_ref[dest] = sums


def again(ref, out_ref):
    for dest in range(8):
        out_ref[dest] = ref[...]


def lay_out(final_ref, *outs):
    for i in range(4):
        for h in range(2):
            for pair in range(4):
                first = final_ref[pair * 2, 7 - i * 2 - h].astype(f32)
                second = final_ref[pair * 2 + 1, 7 - i * 2 - h].astype(f32)
                for a in range(8):
                    both = jnp.concatenate(
                        (first[a * 8 : a * 8 + 8, :], second[a * 8 : a * 8 + 8, :]), 0
                    )
                    outs[i][
                        pair * 16 : pair * 16 + 16, a * 256 + h * 128 : a * 256 + h * 128 + 128
                    ] = both.astype(bf16)


def join_video(own_ref, sent_ref, out_ref):
    logs = [joined(sent_ref[c, 128:144, :].astype(f32)) for c in range(8)]
    best = functools.reduce(jnp.maximum, logs)
    shares = [jnp.exp(log - best) for log in logs]
    total = sum(shares)
    for h in range(2):
        lanes = slice(h * 128, h * 128 + 128)
        result = own_ref[:, lanes]
        for c in range(8):
            column = jnp.transpose(jnp.broadcast_to((shares[c] / total)[:, lanes], (128, 128)))
            result += sent_ref[c, 0:128, lanes].astype(f32) * column
        out_ref[:, lanes] = result.astype(bf16)


def swap(value, axis, distance):
    count = lax.axis_size(axis)
    return lax.ppermute(value, axis, [(i, i ^ distance) for i in range(count)])


def backwards(value, axes):
    order = list(range(value.shape[0]))[::-1]
    return lax.all_to_all(value, axes, 0, 0, axis_index_groups=[order], tiled=True)


def local(
    video_query,
    video_key,
    video_value,
    audio_query,
    audio_key,
    audio_value,
    video_grad,
    audio_grad,
    block_list,
    block_count,
):
    (audio,) = call(
        pack_audio,
        [((8, CHUNK, 256), bf16)],
        10**6,
        scratch=[
            pltpu.VMEM((4, 16, 2048), bf16),
            pltpu.SemaphoreType.DMA((4,)),
        ],
        in_specs=[HBM] * 4,
        limit=60 * 1024 * 1024,
        args=(audio_query, audio_grad, audio_key, audio_value),
    )
    audio = lax.all_to_all(audio, AUD, 0, 0, tiled=True)
    (packed,) = call(
        pack_video,
        [((8, PACK // 16, 16, 256), bf16)],
        10**6,
        scratch=[
            pltpu.VMEM((4, 8, 16, 256), bf16),
            pltpu.VMEM((16, 256), bf16),
            pltpu.SemaphoreType.DMA((44,)),
        ],
        in_specs=[SM, SM] + [HBM] * 4,
        out_specs=[HBM],
        limit=60 * 1024 * 1024,
        args=(
            block_list,
            block_count,
            *(
                matrix.reshape(8, 16, 256)
                for matrix in (video_query, video_key, video_value, video_grad)
            ),
        ),
    )
    diag, packed = call(
        add_audio,
        [((4, 128, 256), bf16), ((8, PACK // 16, 16, 256), bf16)],
        10**6,
        scratch=[pltpu.VMEM((4, 128, 256), f32), pltpu.SemaphoreType.DMA((8,))],
        in_specs=[VM, HBM],
        out_specs=[VM, HBM],
        aliases={1: 1},
        limit=60 * 1024 * 1024,
        args=(audio, packed),
    )
    near = video_query.reshape(1, 128, 256)
    packed, near = lax.optimization_barrier((packed, near))
    packed = lax.all_to_all(packed, ROWS, 0, 0, tiled=True).reshape(8, PACK, 256)
    for distance in (4, 2):
        far = swap(near, "z", distance)
        (near,) = call(
            side_by_side, [((2 * near.shape[0], 128, 256), bf16)], 10**6, args=(near, far)
        )
    far = swap(near, "z", 1)
    (stats,) = call(
        back_stats,
        [((13, 256), f32)],
        10**9,
        scratch=[pltpu.VMEM((8, 128, 128), f32)] * 2,
        args=(packed, diag),
    )
    (sent,) = call(
        self_part,
        [((8, SENT, 256), bf16)],
        4 * 10**9,
        args=(near, far, packed, stats),
    )
    sent = backwards(sent, COLS)
    cross_own, sums = call(
        cross_part,
        [((128, 256), f32), ((2, 128, 128), f32)],
        4 * 10**9,
        scratch=[pltpu.VMEM((8, 128, 256), f32)],
        args=(packed, diag),
    )
    (terms,) = call(
        back_terms,
        [((64, 8, 128), f32)],
        10**9,
        scratch=[
            pltpu.VMEM((2, 128, 256), bf16),
            pltpu.VMEM((2, 128, 128), f32),
            pltpu.SemaphoreType.DMA((2,)),
        ],
        in_specs=[VM, VM, HBM, HBM],
        limit=48 * 1024 * 1024,
        args=(sent, packed, diag, sums),
    )
    terms = backwards(terms, AUD + COLS)
    (video_out,) = call(join_video, [((128, 256), bf16)], 10**7, args=(cross_own, sent))
    (summed,) = call(add_terms, [((8, 64, 128), bf16)], 10**6, args=(terms,))
    final = backwards(summed, COLS)
    (final,) = call(again, [((8, 8, 64, 128), bf16)], 10**6, args=(final,))
    final = lax.all_to_all(final, ROWS, 0, 0, tiled=True)
    finished = call(lay_out, [((64, 2048), bf16)] * 4, 10**6, args=(final,))
    return (video_out, *finished)


def solution(mesh):
    fine = Mesh(mesh.devices.reshape(4, 2, 8, 4, 2), ("x", "yl", "z", "yh", "core"))
    video, audio = P(SEQ, AUD), P(AUD, None)
    return jax.shard_map(
        local,
        mesh=fine,
        in_specs=(
            video,
            video,
            video,
            audio,
            audio,
            audio,
            video,
            audio,
            P(SEQ, None),
            P(SEQ),
        ),
        out_specs=(video, audio, audio, audio, audio),
        check_vma=False,
    )
```

```python
import functools
import math

import jax
import jax.numpy as jnp
from jax import lax
from jax.experimental import pallas as pl
from jax.experimental.pallas import tpu as pltpu
from jax.sharding import Mesh, PartitionSpec as P

HEAD_DIM = 128
ROWS = ("x", "yl")
COLS = ("z",)
AUD = ("yh", "core")
SEQ = ROWS + COLS
SCALE = 1.0 / math.sqrt(HEAD_DIM)
bf16 = jnp.bfloat16
f32 = jnp.float32
VMEM_LIMIT = 20 * 1024 * 1024
PACK = 656
CHUNK = 32
SENT = 144


VM = pl.BlockSpec(memory_space=pltpu.VMEM)
SM = pl.BlockSpec(memory_space=pltpu.SMEM)
HBM = pl.BlockSpec(memory_space=pl.ANY)


def call(
    kernel,
    outs,
    flops,
    scratch=(),
    smem=0,
    args=(),
    in_specs=None,
    out_specs=None,
    limit=VMEM_LIMIT,
    aliases=None,
):
    return pl.pallas_call(
        kernel,
        out_shape=[jax.ShapeDtypeStruct(s, d) for s, d in outs],
        in_specs=in_specs or [SM] * smem + [VM] * (len(args) - smem),
        out_specs=out_specs or [VM] * len(outs),
        scratch_shapes=list(scratch),
        input_output_aliases=aliases or {},
        compiler_params=pltpu.CompilerParams(vmem_limit_bytes=limit),
        cost_estimate=pl.CostEstimate(flops=flops, bytes_accessed=4000000, transcendentals=0),
    )(*args)


def dot_t(left, right):
    return lax.dot_general(left, right, (((1,), (1,)), ((), ())), preferred_element_type=f32)


def dot_n(left, right):
    return lax.dot_general(left, right, (((1,), (0,)), ((), ())), preferred_element_type=f32)


def dot_tn(left, right):
    return lax.dot_general(left, right, (((0,), (0,)), ((), ())), preferred_element_type=f32)


def side_by_side(first_ref, second_ref, out_ref):
    count = first_ref.shape[0]
    out_ref[0:count] = first_ref[...]
    out_ref[count : 2 * count] = second_ref[...]


def pack_video(list_ref, count_ref, *rest):
    ins, out_ref, held, marks, sems = rest[:4], *rest[4:]
    loads = [
        pltpu.make_async_copy(ref, held.at[place], sems.at[place])
        for place, ref in enumerate(ins)
    ]
    for load in loads:
        load.start()
    lanes = lax.broadcasted_iota(jnp.int32, (16, 256), 1)
    block = (lanes % 64) // 16
    allow = jnp.zeros((16, 256), f32)
    for slot in range(3):
        entry = jnp.where(slot < count_ref[0], list_ref[0, slot], -2)
        allow = jnp.where(block == entry, 1.0, allow)
    marks[...] = allow.astype(bf16)
    stores = []
    for dest in range(8):
        stores.append(
            pltpu.make_async_copy(marks, out_ref.at[dest, 32], sems.at[4 + len(stores)])
        )
        stores[-1].start()
    for place, load in enumerate(loads):
        load.wait()
        for dest in range(8):
            target = out_ref.at[dest, place * 8 : place * 8 + 8]
            stores.append(
                pltpu.make_async_copy(held.at[place], target, sems.at[4 + len(stores)])
            )
            stores[-1].start()
    for store in stores:
        store.wait()


def pack_audio(*rest):
    ins, out_ref, held, sems = rest[:4], *rest[4:]
    row = lax.axis_index(ROWS)
    pair = pl.ds(pl.multiple_of(row // 2 * 16, 16), 16)
    loads = [
        pltpu.make_async_copy(ref.at[pair], held.at[place], sems.at[place])
        for place, ref in enumerate(ins)
    ]
    for load in loads:
        load.start()
    parts = []
    for place, load in enumerate(loads):
        load.wait()
        both = held[place].astype(f32)
        parts.append(jnp.where(lax.rem(row, 2) == 0, both[0:8, :], both[8:16, :]))
    parts = jnp.concatenate(parts, 0).astype(bf16)
    for dest in range(8):
        out_ref[7 - dest] = parts[:, dest * 256 : dest * 256 + 256]


def add_audio(audio_ref, given_ref, diag_ref, out_ref, wide_ref, sems):
    stores = [
        pltpu.make_async_copy(audio_ref.at[:, 16:32], out_ref.at[dest, 33:41], sems.at[dest])
        for dest in range(8)
    ]
    for store in stores:
        store.start()
    wide_ref[...] = jnp.zeros((4, 128, 256), f32)
    for source in range(8):
        part = audio_ref[7 - source].astype(f32)
        for place in range(4):
            for h in range(2):
                row, lanes = source * 8 + h * 64, slice(h * 128, h * 128 + 128)
                wide_ref[place, row : row + 8, lanes] = part[place * 8 : place * 8 + 8, lanes]
    diag_ref[...] = wide_ref[...].astype(bf16)
    for store in stores:
        store.wait()


def thirds(whole):
    high = whole.astype(bf16).astype(f32)
    middle = (whole - high).astype(bf16).astype(f32)
    return [high, middle, whole - high - middle]


def joined(rows):
    return rows[0:1, :] + rows[1:2, :] + rows[2:3, :]


def back_stats(packed_ref, diag_ref, stats_ref, score_ref, dprob_ref):
    queries, upstream = diag_ref[0], diag_ref[1]
    best = jnp.full((1, 128), -1e30, f32)
    for r in range(8):
        allowed = packed_ref[r, 512:528, 0:128].astype(f32)[0:1, :] > 0.5
        scores = dot_t(packed_ref[r, 128:256, :], queries) * SCALE
        score_ref[r] = scores
        dprob_ref[r] = dot_t(packed_ref[r, 256:384, :], upstream)
        peak = jnp.max(scores, axis=0, keepdims=True)
        best = jnp.maximum(best, jnp.where(allowed, peak, -1e30))
    total = jnp.zeros((1, 128), f32)
    delta = jnp.zeros((1, 128), f32)
    for r in range(8):
        allowed = packed_ref[r, 512:528, 0:128].astype(f32)[0:1, :] > 0.5
        weights = jnp.where(allowed, jnp.exp(score_ref[r] - best), 0.0)
        total += jnp.sum(weights, axis=0, keepdims=True)
        delta += jnp.sum(weights.astype(bf16).astype(f32) * dprob_ref[r], axis=0, keepdims=True)
    stats = thirds(best) + thirds(total) + thirds(delta) + [jnp.zeros((4, 128), f32)]
    stats = jnp.concatenate(stats, 0)
    stats_ref[...] = jnp.concatenate((stats, jnp.zeros((13, 128), f32)), 1)


def self_part(near_ref, far_ref, packed_ref, stats_ref, out_ref):
    column = lax.axis_index("z")
    for part_ref, distances in ((near_ref, (0, 4, 2, 6)), (far_ref, (1, 5, 3, 7))):
        logs = []
        for h in range(2):
            lanes = slice(h * 128, h * 128 + 128)
            queries = part_ref[:, :, lanes].reshape(512, 128)
            keys = packed_ref[:, 128:256, lanes].reshape(1024, 128)
            values = packed_ref[:, 256:384, lanes].reshape(1024, 128)
            scores = dot_t(queries, keys)
            best = jnp.max(scores, axis=1, keepdims=True)
            weights = jnp.exp2((scores - best) * (SCALE * math.log2(math.e)))
            total = jnp.sum(weights, axis=1, keepdims=True)
            out = dot_n(weights.astype(bf16), values) / total
            out = out.astype(bf16).reshape(4, 128, 128)
            for place, distance in enumerate(distances):
                out_ref[7 - (column ^ distance), 0:128, lanes] = out[place]
            logs.append(jnp.broadcast_to(best * SCALE + jnp.log(total), (512, 128)))
        logs = [jnp.transpose(part)[0:1, :] for part in logs]
        for place, distance in enumerate(distances):
            whole = jnp.concatenate([part[:, place * 128 : place * 128 + 128] for part in logs], 1)
            rows = jnp.concatenate(thirds(whole) + [stats_ref[...]], 0)
            out_ref[7 - (column ^ distance), 128:144, :] = rows.astype(bf16)


def cross_part(
    packed_ref, diag_ref, own_ref, sums_ref, out_ref
):
    diag_key, diag_value = diag_ref[2], diag_ref[3]
    audio = packed_ref[:, 528:656, :].astype(f32).reshape(8, 8, 16, 256)
    audio = jnp.stack([audio[:, 7 - a] for a in range(8)], 1)
    all_keys = audio[:, :, 0:8, :].reshape(512, 256).astype(bf16)
    all_values = audio[:, :, 8:16, :].reshape(512, 256).astype(bf16)
    key_terms = jnp.zeros((128, 256), f32)
    value_terms = jnp.zeros((128, 256), f32)
    for r in range(8):
        allowed = packed_ref[r, 512:528, 0:128].astype(f32)[0:1, :] > 0.5
        queries2, upstream2 = packed_ref[r, 0:128, :], packed_ref[r, 384:512, :]
        stats = []
        for h in range(2):
            lanes = slice(h * 128, h * 128 + 128)
            scores = dot_t(queries2[:, lanes], all_keys[:, lanes]) * SCALE
            parts = [scores[:, b * 128 : b * 128 + 128] for b in range(4)]
            peak = jnp.where(allowed, functools.reduce(jnp.maximum, parts), -jnp.inf)
            best = jnp.max(peak, axis=1, keepdims=True)
            weights = [jnp.where(allowed, jnp.exp(p - best), 0.0) for p in parts]
            total = jnp.sum(sum(weights), axis=1, keepdims=True)
            weights = jnp.concatenate([w.astype(bf16) for w in weights], 1)
            out = dot_n(weights, all_values[:, lanes]) / total
            out_ref[r, :, lanes] = out
            delta = jnp.sum(upstream2[:, lanes].astype(f32) * out, axis=1, keepdims=True)
            stats.append((best, total, delta))
        low_lanes = lax.broadcasted_iota(jnp.int32, (128, 128), 1) < 64
        best, total, delta = [jnp.where(low_lanes, s0, s1) for s0, s1 in zip(*stats)]
        scores = dot_t(queries2, diag_key) * SCALE
        probs = jnp.where(allowed, jnp.exp(scores - best), 0.0) / total
        dscores = probs * (dot_t(upstream2, diag_value) - delta)
        value_terms += dot_tn(probs.astype(bf16), upstream2)
        key_terms += dot_tn(dscores.astype(bf16), queries2)
    for h in range(2):
        rows, lanes = slice(h * 64, h * 64 + 64), slice(h * 128, h * 128 + 128)
        sums_ref[0, rows, :] = key_terms[rows, lanes] * SCALE
        sums_ref[1, rows, :] = value_terms[rows, lanes]
    own_ref[...] = out_ref[lax.axis_index(ROWS)]


def back_terms(
    sent_ref, packed_ref, diag_far_ref, sums_far_ref, out_ref, diag_ref, sums_ref, sems
):
    loads = [
        pltpu.make_async_copy(diag_far_ref.at[0:2], diag_ref, sems.at[0]),
        pltpu.make_async_copy(sums_far_ref, sums_ref, sems.at[1]),
    ]
    for load in loads:
        load.start()
    stats = [sent_ref[c, 128:144, 0:128].astype(f32) for c in range(8)]
    bests = [joined(part[3:6, :]) for part in stats]
    best = functools.reduce(jnp.maximum, bests)
    factors = [jnp.exp(part - best) for part in bests]
    total = sum(joined(part[6:9, :]) * factor for part, factor in zip(stats, factors))
    delta = sum(joined(part[9:12, :]) * factor for part, factor in zip(stats, factors)) / total
    for load in loads:
        load.wait()
    queries, upstream = diag_ref[0], diag_ref[1]
    attn = jnp.zeros((128, 256), f32)
    grads = jnp.zeros((128, 256), f32)
    for r in range(8):
        allowed = packed_ref[r, 512:528, 0:128].astype(f32)[0:1, :] > 0.5
        keys, values = packed_ref[r, 128:256, :], packed_ref[r, 256:384, :]
        weights = jnp.where(allowed, jnp.exp(dot_t(keys, queries) * SCALE - best), 0.0)
        dscores = (weights / total) * (dot_t(values, upstream) - delta)
        attn += dot_tn(weights.astype(bf16), values)
        grads += dot_tn(dscores.astype(bf16), keys)
    totals = jnp.transpose(jnp.broadcast_to(total, (128, 128)))
    attn = jnp.concatenate((attn[:, 0:128] / totals, attn[:, 128:256] / totals), 1)
    grads = grads * SCALE
    for h in range(2):
        lanes = slice(h * 128, h * 128 + 128)
        for a in range(8):
            rows = slice(h * 64 + a * 8, h * 64 + a * 8 + 8)
            out_ref[63 - (a * 8 + h)] = attn[rows, lanes]
            out_ref[63 - (a * 8 + 2 + h)] = grads[rows, lanes]
            out_ref[63 - (a * 8 + 4 + h)] = sums_ref[0, rows, :]
            out_ref[63 - (a * 8 + 6 + h)] = sums_ref[1, rows, :]


def add_terms(terms_ref, out_ref):
    sums = [sum(terms_ref[(7 - a) * 8 + c] for c in range(8)) for a in range(8)]
    sums = jnp.concatenate(sums, 0).astype(bf16)
    for dest in range(8):
        out_ref[dest] = sums


def again(ref, out_ref):
    for dest in range(8):
        out_ref[dest] = ref[...]


def lay_out(final_ref, *outs):
    for i in range(4):
        for h in range(2):
            for pair in range(4):
                first = final_ref[7 - pair * 2, 7 - i * 2 - h].astype(f32)
                second = final_ref[6 - pair * 2, 7 - i * 2 - h].astype(f32)
                for a in range(8):
                    both = jnp.concatenate(
                        (first[a * 8 : a * 8 + 8, :], second[a * 8 : a * 8 + 8, :]), 0
                    )
                    outs[i][
                        pair * 16 : pair * 16 + 16, a * 256 + h * 128 : a * 256 + h * 128 + 128
                    ] = both.astype(bf16)


def join_video(own_ref, sent_ref, out_ref):
    logs = [joined(sent_ref[c, 128:144, :].astype(f32)) for c in range(8)]
    best = functools.reduce(jnp.maximum, logs)
    shares = [jnp.exp(log - best) for log in logs]
    total = sum(shares)
    for h in range(2):
        lanes = slice(h * 128, h * 128 + 128)
        result = own_ref[:, lanes]
        for c in range(8):
            column = jnp.transpose(jnp.broadcast_to((shares[c] / total)[:, lanes], (128, 128)))
            result += sent_ref[c, 0:128, lanes].astype(f32) * column
        out_ref[:, lanes] = result.astype(bf16)


def swap(value, axis, distance):
    count = lax.axis_size(axis)
    return lax.ppermute(value, axis, [(i, i ^ distance) for i in range(count)])


def backwards(value, axes):
    order = list(range(value.shape[0]))[::-1]
    return lax.all_to_all(value, axes, 0, 0, axis_index_groups=[order], tiled=True)


def local(
    video_query,
    video_key,
    video_value,
    audio_query,
    audio_key,
    audio_value,
    video_grad,
    audio_grad,
    block_list,
    block_count,
):
    (audio,) = call(
        pack_audio,
        [((8, CHUNK, 256), bf16)],
        10**6,
        scratch=[
            pltpu.VMEM((4, 16, 2048), bf16),
            pltpu.SemaphoreType.DMA((4,)),
        ],
        in_specs=[HBM] * 4,
        limit=60 * 1024 * 1024,
        args=(audio_query, audio_grad, audio_key, audio_value),
    )
    audio = backwards(audio, AUD)
    (packed,) = call(
        pack_video,
        [((8, PACK // 16, 16, 256), bf16)],
        10**6,
        scratch=[
            pltpu.VMEM((4, 8, 16, 256), bf16),
            pltpu.VMEM((16, 256), bf16),
            pltpu.SemaphoreType.DMA((44,)),
        ],
        in_specs=[SM, SM] + [HBM] * 4,
        out_specs=[HBM],
        limit=60 * 1024 * 1024,
        args=(
            block_list,
            block_count,
            *(
                matrix.reshape(8, 16, 256)
                for matrix in (video_query, video_key, video_value, video_grad)
            ),
        ),
    )
    diag, packed = call(
        add_audio,
        [((4, 128, 256), bf16), ((8, PACK // 16, 16, 256), bf16)],
        10**6,
        scratch=[pltpu.VMEM((4, 128, 256), f32), pltpu.SemaphoreType.DMA((8,))],
        in_specs=[VM, HBM],
        out_specs=[VM, HBM],
        aliases={1: 1},
        limit=60 * 1024 * 1024,
        args=(audio, packed),
    )
    near = video_query.reshape(1, 128, 256)
    packed, near = lax.optimization_barrier((packed, near))
    packed = lax.all_to_all(packed, ROWS, 0, 0, tiled=True).reshape(8, PACK, 256)
    for distance in (4, 2):
        far = swap(near, "z", distance)
        (near,) = call(
            side_by_side, [((2 * near.shape[0], 128, 256), bf16)], 10**6, args=(near, far)
        )
    far = swap(near, "z", 1)
    (stats,) = call(
        back_stats,
        [((13, 256), f32)],
        10**9,
        scratch=[pltpu.VMEM((8, 128, 128), f32)] * 2,
        args=(packed, diag),
    )
    (sent,) = call(
        self_part,
        [((8, SENT, 256), bf16)],
        4 * 10**9,
        args=(near, far, packed, stats),
    )
    sent = backwards(sent, COLS)
    cross_own, sums = call(
        cross_part,
        [((128, 256), f32), ((2, 128, 128), f32)],
        4 * 10**9,
        scratch=[pltpu.VMEM((8, 128, 256), f32)],
        args=(packed, diag),
    )
    (terms,) = call(
        back_terms,
        [((64, 8, 128), f32)],
        10**9,
        scratch=[
            pltpu.VMEM((2, 128, 256), bf16),
            pltpu.VMEM((2, 128, 128), f32),
            pltpu.SemaphoreType.DMA((2,)),
        ],
        in_specs=[VM, VM, HBM, HBM],
        limit=48 * 1024 * 1024,
        args=(sent, packed, diag, sums),
    )
    terms = backwards(terms, AUD + COLS)
    (video_out,) = call(join_video, [((128, 256), bf16)], 10**7, args=(cross_own, sent))
    (summed,) = call(add_terms, [((8, 64, 128), bf16)], 10**6, args=(terms,))
    final = backwards(summed, COLS)
    (final,) = call(again, [((8, 8, 64, 128), bf16)], 10**6, args=(final,))
    final = backwards(final, ROWS)
    finished = call(lay_out, [((64, 2048), bf16)] * 4, 10**6, args=(final,))
    return (video_out, *finished)


def solution(mesh):
    fine = Mesh(mesh.devices.reshape(4, 2, 8, 4, 2), ("x", "yl", "z", "yh", "core"))
    video, audio = P(SEQ, AUD), P(AUD, None)
    return jax.shard_map(
        local,
        mesh=fine,
        in_specs=(
            video,
            video,
            video,
            audio,
            audio,
            audio,
            video,
            audio,
            P(SEQ, None),
            P(SEQ),
        ),
        out_specs=(video, audio, audio, audio, audio),
        check_vma=False,
    )
```

```python
import functools
import math

import jax
import jax.numpy as jnp
from jax import lax
from jax.experimental import pallas as pl
from jax.experimental.pallas import tpu as pltpu
from jax.sharding import Mesh, PartitionSpec as P

HEAD_DIM = 128
ROWS = ("x", "yl")
COLS = ("z",)
AUD = ("yh", "core")
SEQ = ROWS + COLS
SCALE = 1.0 / math.sqrt(HEAD_DIM)
bf16 = jnp.bfloat16
f32 = jnp.float32
VMEM_LIMIT = 20 * 1024 * 1024
PACK = 656
CHUNK = 32
SENT = 144


VM = pl.BlockSpec(memory_space=pltpu.VMEM)
SM = pl.BlockSpec(memory_space=pltpu.SMEM)
HBM = pl.BlockSpec(memory_space=pl.ANY)


def call(
    kernel,
    outs,
    flops,
    scratch=(),
    smem=0,
    args=(),
    in_specs=None,
    out_specs=None,
    limit=VMEM_LIMIT,
    aliases=None,
):
    return pl.pallas_call(
        kernel,
        out_shape=[jax.ShapeDtypeStruct(s, d) for s, d in outs],
        in_specs=in_specs or [SM] * smem + [VM] * (len(args) - smem),
        out_specs=out_specs or [VM] * len(outs),
        scratch_shapes=list(scratch),
        input_output_aliases=aliases or {},
        compiler_params=pltpu.CompilerParams(vmem_limit_bytes=limit),
        cost_estimate=pl.CostEstimate(flops=flops, bytes_accessed=4000000, transcendentals=0),
    )(*args)


def dot_t(left, right):
    return lax.dot_general(left, right, (((1,), (1,)), ((), ())), preferred_element_type=f32)


def dot_n(left, right):
    return lax.dot_general(left, right, (((1,), (0,)), ((), ())), preferred_element_type=f32)


def dot_tn(left, right):
    return lax.dot_general(left, right, (((0,), (0,)), ((), ())), preferred_element_type=f32)


def side_by_side(first_ref, second_ref, out_ref):
    count = first_ref.shape[0]
    out_ref[0:count] = first_ref[...]
    out_ref[count : 2 * count] = second_ref[...]


def pack_video(list_ref, count_ref, *rest):
    ins, out_ref, held, sems = rest[:4], *rest[4:]
    loads = [
        pltpu.make_async_copy(ref, held.at[place * 8 : place * 8 + 8], sems.at[place])
        for place, ref in enumerate(ins)
    ]
    for load in loads:
        load.start()
    lanes = lax.broadcasted_iota(jnp.int32, (16, 256), 1)
    block = (lanes % 64) // 16
    allow = jnp.zeros((16, 256), f32)
    for slot in range(3):
        entry = jnp.where(slot < count_ref[0], list_ref[0, slot], -2)
        allow = jnp.where(block == entry, 1.0, allow)
    held[32] = allow.astype(bf16)
    for load in loads:
        load.wait()
    stores = [
        pltpu.make_async_copy(held, out_ref.at[dest, 0:33], sems.at[4 + dest]) for dest in range(8)
    ]
    for store in stores:
        store.start()
    for store in stores:
        store.wait()


def pack_audio(*rest):
    ins, out_ref, held, sems = rest[:4], *rest[4:]
    row = lax.axis_index(ROWS)
    pair = pl.ds(pl.multiple_of(row // 2 * 16, 16), 16)
    loads = [
        pltpu.make_async_copy(ref.at[pair], held.at[place], sems.at[place])
        for place, ref in enumerate(ins)
    ]
    for load in loads:
        load.start()
    parts = []
    for place, load in enumerate(loads):
        load.wait()
        both = held[place].astype(f32)
        parts.append(jnp.where(lax.rem(row, 2) == 0, both[0:8, :], both[8:16, :]))
    parts = jnp.concatenate(parts, 0).astype(bf16)
    for dest in range(8):
        out_ref[7 - dest] = parts[:, dest * 256 : dest * 256 + 256]


def add_audio(audio_ref, given_ref, diag_ref, out_ref, wide_ref, sems):
    stores = [
        pltpu.make_async_copy(audio_ref.at[:, 16:32], out_ref.at[dest, 33:41], sems.at[dest])
        for dest in range(8)
    ]
    for store in stores:
        store.start()
    wide_ref[...] = jnp.zeros((4, 128, 256), f32)
    for source in range(8):
        part = audio_ref[7 - source].astype(f32)
        for place in range(4):
            for h in range(2):
                row, lanes = source * 8 + h * 64, slice(h * 128, h * 128 + 128)
                wide_ref[place, row : row + 8, lanes] = part[place * 8 : place * 8 + 8, lanes]
    diag_ref[...] = wide_ref[...].astype(bf16)
    for store in stores:
        store.wait()


def thirds(whole):
    high = whole.astype(bf16).astype(f32)
    middle = (whole - high).astype(bf16).astype(f32)
    return [high, middle, whole - high - middle]


def joined(rows):
    return rows[0:1, :] + rows[1:2, :] + rows[2:3, :]


def back_stats(packed_ref, diag_ref, stats_ref, score_ref, dprob_ref):
    queries, upstream = diag_ref[0], diag_ref[1]
    best = jnp.full((1, 128), -1e30, f32)
    for r in range(8):
        allowed = packed_ref[r, 512:528, 0:128].astype(f32)[0:1, :] > 0.5
        scores = dot_t(packed_ref[r, 128:256, :], queries) * SCALE
        score_ref[r] = scores
        dprob_ref[r] = dot_t(packed_ref[r, 256:384, :], upstream)
        peak = jnp.max(scores, axis=0, keepdims=True)
        best = jnp.maximum(best, jnp.where(allowed, peak, -1e30))
    total = jnp.zeros((1, 128), f32)
    delta = jnp.zeros((1, 128), f32)
    for r in range(8):
        allowed = packed_ref[r, 512:528, 0:128].astype(f32)[0:1, :] > 0.5
        weights = jnp.where(allowed, jnp.exp(score_ref[r] - best), 0.0)
        total += jnp.sum(weights, axis=0, keepdims=True)
        delta += jnp.sum(weights.astype(bf16).astype(f32) * dprob_ref[r], axis=0, keepdims=True)
    stats = thirds(best) + thirds(total) + thirds(delta) + [jnp.zeros((4, 128), f32)]
    stats = jnp.concatenate(stats, 0)
    stats_ref[...] = jnp.concatenate((stats, jnp.zeros((13, 128), f32)), 1)


def self_part(near_ref, far_ref, packed_ref, stats_ref, out_ref):
    column = lax.axis_index("z")
    for part_ref, distances in ((near_ref, (0, 4, 2, 6)), (far_ref, (1, 5, 3, 7))):
        logs = []
        for h in range(2):
            lanes = slice(h * 128, h * 128 + 128)
            queries = part_ref[:, :, lanes].reshape(512, 128)
            keys = packed_ref[:, 128:256, lanes].reshape(1024, 128)
            values = packed_ref[:, 256:384, lanes].reshape(1024, 128)
            scores = dot_t(queries, keys)
            best = jnp.max(scores, axis=1, keepdims=True)
            weights = jnp.exp2((scores - best) * (SCALE * math.log2(math.e)))
            total = jnp.sum(weights, axis=1, keepdims=True)
            out = dot_n(weights.astype(bf16), values) / total
            out = out.astype(bf16).reshape(4, 128, 128)
            for place, distance in enumerate(distances):
                out_ref[7 - (column ^ distance), 0:128, lanes] = out[place]
            logs.append(jnp.broadcast_to(best * SCALE + jnp.log(total), (512, 128)))
        logs = [jnp.transpose(part)[0:1, :] for part in logs]
        for place, distance in enumerate(distances):
            whole = jnp.concatenate([part[:, place * 128 : place * 128 + 128] for part in logs], 1)
            rows = jnp.concatenate(thirds(whole) + [stats_ref[...]], 0)
            out_ref[7 - (column ^ distance), 128:144, :] = rows.astype(bf16)


def cross_part(
    packed_ref, diag_ref, own_ref, sums_ref, out_ref
):
    diag_key, diag_value = diag_ref[2], diag_ref[3]
    audio = packed_ref[:, 528:656, :].astype(f32).reshape(8, 8, 16, 256)
    audio = jnp.stack([audio[:, 7 - a] for a in range(8)], 1)
    all_keys = audio[:, :, 0:8, :].reshape(512, 256).astype(bf16)
    all_values = audio[:, :, 8:16, :].reshape(512, 256).astype(bf16)
    key_terms = jnp.zeros((128, 256), f32)
    value_terms = jnp.zeros((128, 256), f32)
    for r in range(8):
        allowed = packed_ref[r, 512:528, 0:128].astype(f32)[0:1, :] > 0.5
        queries2, upstream2 = packed_ref[r, 0:128, :], packed_ref[r, 384:512, :]
        stats = []
        for h in range(2):
            lanes = slice(h * 128, h * 128 + 128)
            scores = dot_t(queries2[:, lanes], all_keys[:, lanes]) * SCALE
            parts = [scores[:, b * 128 : b * 128 + 128] for b in range(4)]
            peak = jnp.where(allowed, functools.reduce(jnp.maximum, parts), -jnp.inf)
            best = jnp.max(peak, axis=1, keepdims=True)
            weights = [jnp.where(allowed, jnp.exp(p - best), 0.0) for p in parts]
            total = jnp.sum(sum(weights), axis=1, keepdims=True)
            weights = jnp.concatenate([w.astype(bf16) for w in weights], 1)
            out = dot_n(weights, all_values[:, lanes]) / total
            out_ref[r, :, lanes] = out
            delta = jnp.sum(upstream2[:, lanes].astype(f32) * out, axis=1, keepdims=True)
            stats.append((best, total, delta))
        low_lanes = lax.broadcasted_iota(jnp.int32, (128, 128), 1) < 64
        best, total, delta = [jnp.where(low_lanes, s0, s1) for s0, s1 in zip(*stats)]
        scores = dot_t(queries2, diag_key) * SCALE
        probs = jnp.where(allowed, jnp.exp(scores - best), 0.0) / total
        dscores = probs * (dot_t(upstream2, diag_value) - delta)
        value_terms += dot_tn(probs.astype(bf16), upstream2)
        key_terms += dot_tn(dscores.astype(bf16), queries2)
    for h in range(2):
        rows, lanes = slice(h * 64, h * 64 + 64), slice(h * 128, h * 128 + 128)
        sums_ref[0, rows, :] = key_terms[rows, lanes] * SCALE
        sums_ref[1, rows, :] = value_terms[rows, lanes]
    own_ref[...] = out_ref[7 - lax.axis_index(ROWS)]


def back_terms(
    sent_ref, packed_ref, diag_far_ref, sums_far_ref, out_ref, diag_ref, sums_ref, sems
):
    loads = [
        pltpu.make_async_copy(diag_far_ref.at[0:2], diag_ref, sems.at[0]),
        pltpu.make_async_copy(sums_far_ref, sums_ref, sems.at[1]),
    ]
    for load in loads:
        load.start()
    stats = [sent_ref[c, 128:144, 0:128].astype(f32) for c in range(8)]
    bests = [joined(part[3:6, :]) for part in stats]
    best = functools.reduce(jnp.maximum, bests)
    factors = [jnp.exp(part - best) for part in bests]
    total = sum(joined(part[6:9, :]) * factor for part, factor in zip(stats, factors))
    delta = sum(joined(part[9:12, :]) * factor for part, factor in zip(stats, factors)) / total
    for load in loads:
        load.wait()
    queries, upstream = diag_ref[0], diag_ref[1]
    attn = jnp.zeros((128, 256), f32)
    grads = jnp.zeros((128, 256), f32)
    for r in range(8):
        allowed = packed_ref[r, 512:528, 0:128].astype(f32)[0:1, :] > 0.5
        keys, values = packed_ref[r, 128:256, :], packed_ref[r, 256:384, :]
        weights = jnp.where(allowed, jnp.exp(dot_t(keys, queries) * SCALE - best), 0.0)
        dscores = (weights / total) * (dot_t(values, upstream) - delta)
        attn += dot_tn(weights.astype(bf16), values)
        grads += dot_tn(dscores.astype(bf16), keys)
    totals = jnp.transpose(jnp.broadcast_to(total, (128, 128)))
    attn = jnp.concatenate((attn[:, 0:128] / totals, attn[:, 128:256] / totals), 1)
    grads = grads * SCALE
    for h in range(2):
        lanes = slice(h * 128, h * 128 + 128)
        for a in range(8):
            rows = slice(h * 64 + a * 8, h * 64 + a * 8 + 8)
            out_ref[63 - (a * 8 + h)] = attn[rows, lanes]
            out_ref[63 - (a * 8 + 2 + h)] = grads[rows, lanes]
            out_ref[63 - (a * 8 + 4 + h)] = sums_ref[0, rows, :]
            out_ref[63 - (a * 8 + 6 + h)] = sums_ref[1, rows, :]


def add_terms(terms_ref, out_ref):
    sums = [sum(terms_ref[(7 - a) * 8 + c] for c in range(8)) for a in range(8)]
    sums = jnp.concatenate(sums, 0).astype(bf16)
    for dest in range(8):
        out_ref[dest] = sums


def again(ref, out_ref):
    for dest in range(8):
        out_ref[dest] = ref[...]


def lay_out(final_ref, *outs):
    for i in range(4):
        for h in range(2):
            for pair in range(4):
                first = final_ref[7 - pair * 2, 7 - i * 2 - h].astype(f32)
                second = final_ref[6 - pair * 2, 7 - i * 2 - h].astype(f32)
                for a in range(8):
                    both = jnp.concatenate(
                        (first[a * 8 : a * 8 + 8, :], second[a * 8 : a * 8 + 8, :]), 0
                    )
                    outs[i][
                        pair * 16 : pair * 16 + 16, a * 256 + h * 128 : a * 256 + h * 128 + 128
                    ] = both.astype(bf16)


def join_video(own_ref, sent_ref, out_ref):
    logs = [joined(sent_ref[c, 128:144, :].astype(f32)) for c in range(8)]
    best = functools.reduce(jnp.maximum, logs)
    shares = [jnp.exp(log - best) for log in logs]
    total = sum(shares)
    for h in range(2):
        lanes = slice(h * 128, h * 128 + 128)
        result = own_ref[:, lanes]
        for c in range(8):
            column = jnp.transpose(jnp.broadcast_to((shares[c] / total)[:, lanes], (128, 128)))
            result += sent_ref[c, 0:128, lanes].astype(f32) * column
        out_ref[:, lanes] = result.astype(bf16)


def swap(value, axis, distance):
    count = lax.axis_size(axis)
    return lax.ppermute(value, axis, [(i, i ^ distance) for i in range(count)])


def backwards(value, axes):
    order = list(range(value.shape[0]))[::-1]
    return lax.all_to_all(value, axes, 0, 0, axis_index_groups=[order], tiled=True)


def local(
    video_query,
    video_key,
    video_value,
    audio_query,
    audio_key,
    audio_value,
    video_grad,
    audio_grad,
    block_list,
    block_count,
):
    (audio,) = call(
        pack_audio,
        [((8, CHUNK, 256), bf16)],
        10**6,
        scratch=[
            pltpu.VMEM((4, 16, 2048), bf16),
            pltpu.SemaphoreType.DMA((4,)),
        ],
        in_specs=[HBM] * 4,
        limit=60 * 1024 * 1024,
        args=(audio_query, audio_grad, audio_key, audio_value),
    )
    audio = backwards(audio, AUD)
    (packed,) = call(
        pack_video,
        [((8, PACK // 16, 16, 256), bf16)],
        10**6,
        scratch=[
            pltpu.VMEM((33, 16, 256), bf16),
            pltpu.SemaphoreType.DMA((12,)),
        ],
        in_specs=[SM, SM] + [HBM] * 4,
        out_specs=[HBM],
        limit=60 * 1024 * 1024,
        args=(
            block_list,
            block_count,
            *(
                matrix.reshape(8, 16, 256)
                for matrix in (video_query, video_key, video_value, video_grad)
            ),
        ),
    )
    diag, packed = call(
        add_audio,
        [((4, 128, 256), bf16), ((8, PACK // 16, 16, 256), bf16)],
        10**6,
        scratch=[pltpu.VMEM((4, 128, 256), f32), pltpu.SemaphoreType.DMA((8,))],
        in_specs=[VM, HBM],
        out_specs=[VM, HBM],
        aliases={1: 1},
        limit=60 * 1024 * 1024,
        args=(audio, packed),
    )
    near = video_query.reshape(1, 128, 256)
    packed, near = lax.optimization_barrier((packed, near))
    packed = backwards(packed, ROWS).reshape(8, PACK, 256)
    for distance in (4, 2):
        far = swap(near, "z", distance)
        (near,) = call(
            side_by_side, [((2 * near.shape[0], 128, 256), bf16)], 10**6, args=(near, far)
        )
    far = swap(near, "z", 1)
    (stats,) = call(
        back_stats,
        [((13, 256), f32)],
        10**9,
        scratch=[pltpu.VMEM((8, 128, 128), f32)] * 2,
        args=(packed, diag),
    )
    (sent,) = call(
        self_part,
        [((8, SENT, 256), bf16)],
        4 * 10**9,
        args=(near, far, packed, stats),
    )
    sent = backwards(sent, COLS)
    cross_own, sums = call(
        cross_part,
        [((128, 256), f32), ((2, 128, 128), f32)],
        4 * 10**9,
        scratch=[pltpu.VMEM((8, 128, 256), f32)],
        args=(packed, diag),
    )
    (terms,) = call(
        back_terms,
        [((64, 8, 128), f32)],
        10**9,
        scratch=[
            pltpu.VMEM((2, 128, 256), bf16),
            pltpu.VMEM((2, 128, 128), f32),
            pltpu.SemaphoreType.DMA((2,)),
        ],
        in_specs=[VM, VM, HBM, HBM],
        limit=48 * 1024 * 1024,
        args=(sent, packed, diag, sums),
    )
    terms = backwards(terms, AUD + COLS)
    (video_out,) = call(join_video, [((128, 256), bf16)], 10**7, args=(cross_own, sent))
    (summed,) = call(add_terms, [((8, 64, 128), bf16)], 10**6, args=(terms,))
    final = backwards(summed, COLS)
    (final,) = call(again, [((8, 8, 64, 128), bf16)], 10**6, args=(final,))
    final = backwards(final, ROWS)
    finished = call(lay_out, [((64, 2048), bf16)] * 4, 10**6, args=(final,))
    return (video_out, *finished)


def solution(mesh):
    fine = Mesh(mesh.devices.reshape(4, 2, 8, 4, 2), ("x", "yl", "z", "yh", "core"))
    video, audio = P(SEQ, AUD), P(AUD, None)
    return jax.shard_map(
        local,
        mesh=fine,
        in_specs=(
            video,
            video,
            video,
            audio,
            audio,
            audio,
            video,
            audio,
            P(SEQ, None),
            P(SEQ),
        ),
        out_specs=(video, audio, audio, audio, audio),
        check_vma=False,
    )
```

```python
import functools
import math

import jax
import jax.numpy as jnp
from jax import lax
from jax.experimental import pallas as pl
from jax.experimental.pallas import tpu as pltpu
from jax.sharding import Mesh, PartitionSpec as P

HEAD_DIM = 128
ROWS = ("x", "yl")
COLS = ("z",)
AUD = ("yh", "core")
SEQ = ROWS + COLS
SCALE = 1.0 / math.sqrt(HEAD_DIM)
bf16 = jnp.bfloat16
f32 = jnp.float32
VMEM_LIMIT = 20 * 1024 * 1024
PACK = 656
CHUNK = 32
SENT = 144


VM = pl.BlockSpec(memory_space=pltpu.VMEM)
SM = pl.BlockSpec(memory_space=pltpu.SMEM)
HBM = pl.BlockSpec(memory_space=pl.ANY)


def call(
    kernel,
    outs,
    flops,
    scratch=(),
    smem=0,
    args=(),
    in_specs=None,
    out_specs=None,
    limit=VMEM_LIMIT,
    aliases=None,
):
    return pl.pallas_call(
        kernel,
        out_shape=[jax.ShapeDtypeStruct(s, d) for s, d in outs],
        in_specs=in_specs or [SM] * smem + [VM] * (len(args) - smem),
        out_specs=out_specs or [VM] * len(outs),
        scratch_shapes=list(scratch),
        input_output_aliases=aliases or {},
        compiler_params=pltpu.CompilerParams(vmem_limit_bytes=limit),
        cost_estimate=pl.CostEstimate(flops=flops, bytes_accessed=4000000, transcendentals=0),
    )(*args)


def dot_t(left, right):
    return lax.dot_general(left, right, (((1,), (1,)), ((), ())), preferred_element_type=f32)


def dot_n(left, right):
    return lax.dot_general(left, right, (((1,), (0,)), ((), ())), preferred_element_type=f32)


def dot_tn(left, right):
    return lax.dot_general(left, right, (((0,), (0,)), ((), ())), preferred_element_type=f32)


def side_by_side(first_ref, second_ref, out_ref):
    count = first_ref.shape[0]
    out_ref[0:count] = first_ref[...]
    out_ref[count : 2 * count] = second_ref[...]


def pack_video(list_ref, count_ref, *rest):
    ins, out_ref, held, sems = rest[:4], *rest[4:]
    loads = [
        pltpu.make_async_copy(ref, held.at[place * 8 : place * 8 + 8], sems.at[place])
        for place, ref in enumerate(ins)
    ]
    for load in loads:
        load.start()
    lanes = lax.broadcasted_iota(jnp.int32, (16, 256), 1)
    block = (lanes % 64) // 16
    allow = jnp.zeros((16, 256), f32)
    for slot in range(3):
        entry = jnp.where(slot < count_ref[0], list_ref[0, slot], -2)
        allow = jnp.where(block == entry, 1.0, allow)
    held[32] = allow.astype(bf16)
    for load in loads:
        load.wait()
    stores = [
        pltpu.make_async_copy(held, out_ref.at[dest, 0:33], sems.at[4 + dest]) for dest in range(8)
    ]
    for store in stores:
        store.start()
    for store in stores:
        store.wait()


def pack_audio(*rest):
    ins, out_ref, held, sems = rest[:4], *rest[4:]
    row = lax.axis_index(ROWS)
    pair = pl.ds(pl.multiple_of(row // 2 * 16, 16), 16)
    loads = [
        pltpu.make_async_copy(ref.at[pair], held.at[place], sems.at[place])
        for place, ref in enumerate(ins)
    ]
    for load in loads:
        load.start()
    parts = []
    for place, load in enumerate(loads):
        load.wait()
        both = held[place].astype(f32)
        parts.append(jnp.where(lax.rem(row, 2) == 0, both[0:8, :], both[8:16, :]))
    parts = jnp.concatenate(parts, 0).astype(bf16)
    for dest in range(8):
        out_ref[7 - dest] = parts[:, dest * 256 : dest * 256 + 256]


def add_audio(audio_ref, given_ref, diag_ref, out_ref, wide_ref, sems):
    stores = [
        pltpu.make_async_copy(audio_ref.at[:, 16:32], out_ref.at[dest, 33:41], sems.at[dest])
        for dest in range(8)
    ]
    for store in stores:
        store.start()
    wide_ref[...] = jnp.zeros((4, 128, 256), f32)
    for source in range(8):
        part = audio_ref[7 - source].astype(f32)
        for place in range(4):
            for h in range(2):
                row, lanes = source * 8 + h * 64, slice(h * 128, h * 128 + 128)
                wide_ref[place, row : row + 8, lanes] = part[place * 8 : place * 8 + 8, lanes]
    diag_ref[...] = wide_ref[...].astype(bf16)
    for store in stores:
        store.wait()


def thirds(whole):
    high = whole.astype(bf16).astype(f32)
    middle = (whole - high).astype(bf16).astype(f32)
    return [high, middle, whole - high - middle]


def joined(rows):
    return rows[0:1, :] + rows[1:2, :] + rows[2:3, :]


def back_stats(packed_ref, diag_ref, stats_ref, score_ref, dprob_ref):
    queries, upstream = diag_ref[0], diag_ref[1]
    best = jnp.full((1, 128), -1e30, f32)
    for r in range(8):
        allowed = packed_ref[r, 512:528, 0:128].astype(f32)[0:1, :] > 0.5
        scores = dot_t(packed_ref[r, 128:256, :], queries) * SCALE
        score_ref[r] = scores
        dprob_ref[r] = dot_t(packed_ref[r, 256:384, :], upstream)
        peak = jnp.max(scores, axis=0, keepdims=True)
        best = jnp.maximum(best, jnp.where(allowed, peak, -1e30))
    total = jnp.zeros((1, 128), f32)
    delta = jnp.zeros((1, 128), f32)
    for r in range(8):
        allowed = packed_ref[r, 512:528, 0:128].astype(f32)[0:1, :] > 0.5
        weights = jnp.where(allowed, jnp.exp(score_ref[r] - best), 0.0)
        total += jnp.sum(weights, axis=0, keepdims=True)
        delta += jnp.sum(weights.astype(bf16).astype(f32) * dprob_ref[r], axis=0, keepdims=True)
    stats = thirds(best) + thirds(total) + thirds(delta) + [jnp.zeros((4, 128), f32)]
    stats = jnp.concatenate(stats, 0)
    stats_ref[...] = jnp.concatenate((stats, jnp.zeros((13, 128), f32)), 1)


def self_part(near_ref, far_ref, packed_ref, stats_ref, out_ref):
    column = lax.axis_index("z")
    for part_ref, distances in ((near_ref, (0, 4, 2, 6)), (far_ref, (1, 5, 3, 7))):
        logs = []
        for h in range(2):
            lanes = slice(h * 128, h * 128 + 128)
            queries = part_ref[:, :, lanes].reshape(512, 128)
            keys = packed_ref[:, 128:256, lanes].reshape(1024, 128)
            values = packed_ref[:, 256:384, lanes].reshape(1024, 128)
            scores = dot_t(queries, keys)
            best = jnp.max(scores, axis=1, keepdims=True)
            weights = jnp.exp2((scores - best) * (SCALE * math.log2(math.e)))
            total = jnp.sum(weights, axis=1, keepdims=True)
            out = dot_n(weights.astype(bf16), values) / total
            out = out.astype(bf16).reshape(4, 128, 128)
            for place, distance in enumerate(distances):
                out_ref[7 - (column ^ distance), 0:128, lanes] = out[place]
            logs.append(jnp.broadcast_to(best * SCALE + jnp.log(total), (512, 128)))
        logs = [jnp.transpose(part)[0:1, :] for part in logs]
        for place, distance in enumerate(distances):
            whole = jnp.concatenate([part[:, place * 128 : place * 128 + 128] for part in logs], 1)
            rows = jnp.concatenate(thirds(whole) + [stats_ref[...]], 0)
            out_ref[7 - (column ^ distance), 128:144, :] = rows.astype(bf16)


def cross_part(
    packed_ref, diag_ref, own_ref, sums_ref, out_ref
):
    diag_key, diag_value = diag_ref[2], diag_ref[3]
    audio = packed_ref[:, 528:656, :].astype(f32).reshape(8, 8, 16, 256)
    audio = jnp.stack([audio[:, 7 - a] for a in range(8)], 1)
    all_keys = audio[:, :, 0:8, :].reshape(512, 256).astype(bf16)
    all_values = audio[:, :, 8:16, :].reshape(512, 256).astype(bf16)
    key_terms = jnp.zeros((128, 256), f32)
    value_terms = jnp.zeros((128, 256), f32)
    for r in range(8):
        allowed = packed_ref[r, 512:528, 0:128].astype(f32)[0:1, :] > 0.5
        queries2, upstream2 = packed_ref[r, 0:128, :], packed_ref[r, 384:512, :]
        stats = []
        for h in range(2):
            lanes = slice(h * 128, h * 128 + 128)
            scores = dot_t(queries2[:, lanes], all_keys[:, lanes]) * SCALE
            parts = [scores[:, b * 128 : b * 128 + 128] for b in range(4)]
            peak = jnp.where(allowed, functools.reduce(jnp.maximum, parts), -jnp.inf)
            best = jnp.max(peak, axis=1, keepdims=True)
            weights = [jnp.where(allowed, jnp.exp(p - best), 0.0) for p in parts]
            total = jnp.sum(sum(weights), axis=1, keepdims=True)
            weights = jnp.concatenate([w.astype(bf16) for w in weights], 1)
            out = dot_n(weights, all_values[:, lanes]) / total
            out_ref[r, :, lanes] = out
            delta = jnp.sum(upstream2[:, lanes].astype(f32) * out, axis=1, keepdims=True)
            stats.append((best, total, delta))
        low_lanes = lax.broadcasted_iota(jnp.int32, (128, 128), 1) < 64
        best, total, delta = [jnp.where(low_lanes, s0, s1) for s0, s1 in zip(*stats)]
        scores = dot_t(queries2, diag_key) * SCALE
        probs = jnp.where(allowed, jnp.exp(scores - best), 0.0) / total
        dscores = probs * (dot_t(upstream2, diag_value) - delta)
        value_terms += dot_tn(probs.astype(bf16), upstream2)
        key_terms += dot_tn(dscores.astype(bf16), queries2)
    for h in range(2):
        rows, lanes = slice(h * 64, h * 64 + 64), slice(h * 128, h * 128 + 128)
        sums_ref[0, rows, :] = key_terms[rows, lanes] * SCALE
        sums_ref[1, rows, :] = value_terms[rows, lanes]
    own_ref[...] = out_ref[lax.axis_index(ROWS)]


def back_terms(
    sent_ref, packed_ref, diag_far_ref, sums_far_ref, out_ref, diag_ref, sums_ref, sems
):
    loads = [
        pltpu.make_async_copy(diag_far_ref.at[0:2], diag_ref, sems.at[0]),
        pltpu.make_async_copy(sums_far_ref, sums_ref, sems.at[1]),
    ]
    for load in loads:
        load.start()
    stats = [sent_ref[c, 128:144, 0:128].astype(f32) for c in range(8)]
    bests = [joined(part[3:6, :]) for part in stats]
    best = functools.reduce(jnp.maximum, bests)
    factors = [jnp.exp(part - best) for part in bests]
    total = sum(joined(part[6:9, :]) * factor for part, factor in zip(stats, factors))
    delta = sum(joined(part[9:12, :]) * factor for part, factor in zip(stats, factors)) / total
    for load in loads:
        load.wait()
    queries, upstream = diag_ref[0], diag_ref[1]
    attn = jnp.zeros((128, 256), f32)
    grads = jnp.zeros((128, 256), f32)
    for r in range(8):
        allowed = packed_ref[r, 512:528, 0:128].astype(f32)[0:1, :] > 0.5
        keys, values = packed_ref[r, 128:256, :], packed_ref[r, 256:384, :]
        weights = jnp.where(allowed, jnp.exp(dot_t(keys, queries) * SCALE - best), 0.0)
        dscores = (weights / total) * (dot_t(values, upstream) - delta)
        attn += dot_tn(weights.astype(bf16), values)
        grads += dot_tn(dscores.astype(bf16), keys)
    totals = jnp.transpose(jnp.broadcast_to(total, (128, 128)))
    attn = jnp.concatenate((attn[:, 0:128] / totals, attn[:, 128:256] / totals), 1)
    grads = grads * SCALE
    for h in range(2):
        lanes = slice(h * 128, h * 128 + 128)
        for a in range(8):
            rows = slice(h * 64 + a * 8, h * 64 + a * 8 + 8)
            out_ref[63 - (a * 8 + h)] = attn[rows, lanes]
            out_ref[63 - (a * 8 + 2 + h)] = grads[rows, lanes]
            out_ref[63 - (a * 8 + 4 + h)] = sums_ref[0, rows, :]
            out_ref[63 - (a * 8 + 6 + h)] = sums_ref[1, rows, :]


def add_terms(terms_ref, out_ref):
    sums = [sum(terms_ref[(7 - a) * 8 + c] for c in range(8)) for a in range(8)]
    sums = jnp.concatenate(sums, 0).astype(bf16)
    for dest in range(8):
        out_ref[dest] = sums


def again(ref, out_ref):
    for dest in range(8):
        out_ref[dest] = ref[...]


def lay_out(final_ref, *outs):
    for i in range(4):
        for h in range(2):
            for pair in range(4):
                first = final_ref[7 - pair * 2, 7 - i * 2 - h].astype(f32)
                second = final_ref[6 - pair * 2, 7 - i * 2 - h].astype(f32)
                for a in range(8):
                    both = jnp.concatenate(
                        (first[a * 8 : a * 8 + 8, :], second[a * 8 : a * 8 + 8, :]), 0
                    )
                    outs[i][
                        pair * 16 : pair * 16 + 16, a * 256 + h * 128 : a * 256 + h * 128 + 128
                    ] = both.astype(bf16)


def join_video(own_ref, sent_ref, out_ref):
    logs = [joined(sent_ref[c, 128:144, :].astype(f32)) for c in range(8)]
    best = functools.reduce(jnp.maximum, logs)
    shares = [jnp.exp(log - best) for log in logs]
    total = sum(shares)
    for h in range(2):
        lanes = slice(h * 128, h * 128 + 128)
        result = own_ref[:, lanes]
        for c in range(8):
            column = jnp.transpose(jnp.broadcast_to((shares[c] / total)[:, lanes], (128, 128)))
            result += sent_ref[c, 0:128, lanes].astype(f32) * column
        out_ref[:, lanes] = result.astype(bf16)


def swap(value, axis, distance):
    count = lax.axis_size(axis)
    return lax.ppermute(value, axis, [(i, i ^ distance) for i in range(count)])


def backwards(value, axes):
    order = list(range(value.shape[0]))[::-1]
    return lax.all_to_all(value, axes, 0, 0, axis_index_groups=[order], tiled=True)


def local(
    video_query,
    video_key,
    video_value,
    audio_query,
    audio_key,
    audio_value,
    video_grad,
    audio_grad,
    block_list,
    block_count,
):
    (audio,) = call(
        pack_audio,
        [((8, CHUNK, 256), bf16)],
        10**6,
        scratch=[
            pltpu.VMEM((4, 16, 2048), bf16),
            pltpu.SemaphoreType.DMA((4,)),
        ],
        in_specs=[HBM] * 4,
        limit=60 * 1024 * 1024,
        args=(audio_query, audio_grad, audio_key, audio_value),
    )
    audio = backwards(audio, AUD)
    (packed,) = call(
        pack_video,
        [((8, PACK // 16, 16, 256), bf16)],
        10**6,
        scratch=[
            pltpu.VMEM((33, 16, 256), bf16),
            pltpu.SemaphoreType.DMA((12,)),
        ],
        in_specs=[SM, SM] + [HBM] * 4,
        out_specs=[HBM],
        limit=60 * 1024 * 1024,
        args=(
            block_list,
            block_count,
            *(
                matrix.reshape(8, 16, 256)
                for matrix in (video_query, video_key, video_value, video_grad)
            ),
        ),
    )
    diag, packed = call(
        add_audio,
        [((4, 128, 256), bf16), ((8, PACK // 16, 16, 256), bf16)],
        10**6,
        scratch=[pltpu.VMEM((4, 128, 256), f32), pltpu.SemaphoreType.DMA((8,))],
        in_specs=[VM, HBM],
        out_specs=[VM, HBM],
        aliases={1: 1},
        limit=60 * 1024 * 1024,
        args=(audio, packed),
    )
    near = video_query.reshape(1, 128, 256)
    packed, near = lax.optimization_barrier((packed, near))
    packed = lax.all_to_all(packed, ROWS, 0, 0, tiled=True).reshape(8, PACK, 256)
    for distance in (4, 2):
        far = swap(near, "z", distance)
        (near,) = call(
            side_by_side, [((2 * near.shape[0], 128, 256), bf16)], 10**6, args=(near, far)
        )
    far = swap(near, "z", 1)
    (stats,) = call(
        back_stats,
        [((13, 256), f32)],
        10**9,
        scratch=[pltpu.VMEM((8, 128, 128), f32)] * 2,
        args=(packed, diag),
    )
    (sent,) = call(
        self_part,
        [((8, SENT, 256), bf16)],
        4 * 10**9,
        args=(near, far, packed, stats),
    )
    sent = backwards(sent, COLS)
    cross_own, sums = call(
        cross_part,
        [((128, 256), f32), ((2, 128, 128), f32)],
        4 * 10**9,
        scratch=[pltpu.VMEM((8, 128, 256), f32)],
        args=(packed, diag),
    )
    (terms,) = call(
        back_terms,
        [((64, 8, 128), f32)],
        10**9,
        scratch=[
            pltpu.VMEM((2, 128, 256), bf16),
            pltpu.VMEM((2, 128, 128), f32),
            pltpu.SemaphoreType.DMA((2,)),
        ],
        in_specs=[VM, VM, HBM, HBM],
        limit=48 * 1024 * 1024,
        args=(sent, packed, diag, sums),
    )
    terms = backwards(terms, AUD + COLS)
    (video_out,) = call(join_video, [((128, 256), bf16)], 10**7, args=(cross_own, sent))
    (summed,) = call(add_terms, [((8, 64, 128), bf16)], 10**6, args=(terms,))
    final = backwards(summed, COLS)
    (final,) = call(again, [((8, 8, 64, 128), bf16)], 10**6, args=(final,))
    final = backwards(final, ROWS)
    finished = call(lay_out, [((64, 2048), bf16)] * 4, 10**6, args=(final,))
    return (video_out, *finished)


def solution(mesh):
    fine = Mesh(mesh.devices.reshape(4, 2, 8, 4, 2), ("x", "yl", "z", "yh", "core"))
    video, audio = P(SEQ, AUD), P(AUD, None)
    return jax.shard_map(
        local,
        mesh=fine,
        in_specs=(
            video,
            video,
            video,
            audio,
            audio,
            audio,
            video,
            audio,
            P(SEQ, None),
            P(SEQ),
        ),
        out_specs=(video, audio, audio, audio, audio),
        check_vma=False,
    )
```
